32 devices in a mesh: gx: 8 (over y, x, core), gy: 4 (over z).
Axes of the slice: x: 2, y: 2, z: 4, core: 2. Of those that a mesh axis runs over, the one named last changes fastest.
Arguments:
- fields: float32 [14, 48, 128, 512], P(None, None, 'gx', 'gy'), may hold values from -1.5 to 9, as said below
- register: float32 [14, 48, 128, 512], P(None, None, 'gx', 'gy'), may hold values from -0.15 to 0.15
Outputs:
- fields_next: float32 [14, 48, 128, 512], P(None, None, 'gx', 'gy')
- register_next: float32 [14, 48, 128, 512], P(None, None, 'gx', 'gy')
- flame_metrics: bfloat16 [5, 48, 128, 512], P(None, 'gy', 'gx')
The draws below stay inside these ranges and needn't reach their ends.
Inputs may be any that keep to these rules, and one draw needn't show every extreme that they name: fields[0] lies in 0.5 to 1.5; velocities fields[1:4] / fields[0] lie within -1 to 1; fields[4] / fields[0] minus half the squared speed lies in 1 to 4; each species density over fields[0] lies in 0.01 to 0.7.
All inputs are finite; a program needn't handle non-finite values.
Results may differ from the reference program's by a relative error of at most 0.0014.
The reference program's roundings to bfloat16 on the way (of `probe`) count: a program that leaves them out, or rounds other values in their place, can miss the bound.
Values may be sent and summed in bfloat16 or wider, within the bound.
No kernel may reach another device: no remote copies, remote signals or barrier semaphores. Data moves between devices by JAX's collectives and lax.ppermute only.
A program may use at most 192 MiB of HBM per device.

```python
import math
import jax
import jax.numpy as jnp
import numpy as np
from jax import lax

FIELDS = 14
CX = 16
CY = 128
Z = 48
NX = 128
NY = 512


def wave_stack(key, count, weights):
    phases = jax.random.uniform(key, (3, count, 1, 1, 1), jnp.float32, 0.0, 2.0 * math.pi)
    turns_first = max(NX // (2 * CX), 1)
    turns_second = max(NY // (2 * CY), 1)
    depth = jnp.arange(Z, dtype=jnp.float32).reshape(1, Z, 1, 1)
    across = jnp.arange(NX, dtype=jnp.float32).reshape(1, 1, NX, 1)
    lengthwise = jnp.arange(NY, dtype=jnp.float32).reshape(1, 1, 1, NY)
    first = jnp.sin(across * (2.0 * math.pi * turns_first / NX) + phases[0])
    second = jnp.sin(lengthwise * (2.0 * math.pi * turns_second / NY) + phases[1])
    third = jnp.sin(depth * (2.0 * math.pi / Z) + phases[2])
    return weights[0] * first + weights[1] * second + weights[2] * third


def draw_fields(key, part):
    key = jax.random.fold_in(key, 7)
    keys = jax.random.split(key, 11)
    grid = (Z, NX, NY)
    weights = (0.5, 0.3, 0.2)
    density_noise = jax.random.uniform(keys[1], (1,) + grid, jnp.float32, -1.0, 1.0)
    speed_noise = jax.random.uniform(keys[4], (3,) + grid, jnp.float32, -1.0, 1.0)
    heat_noise = jax.random.uniform(keys[7], (1,) + grid, jnp.float32, -1.0, 1.0)
    species_noise = jax.random.uniform(keys[10], (9,) + grid, jnp.float32, -1.0, 1.0)
    density = (1.0 + 0.2 * wave_stack(keys[0], 1, weights) + 0.02 * density_noise)[0]
    means = jnp.asarray([0.6, 0.45, 0.0], jnp.float32).reshape(3, 1, 1, 1)
    velocity = means + 0.3 * wave_stack(keys[3], 3, weights) + 0.03 * speed_noise
    internal = (1.7 + 0.5 * wave_stack(keys[6], 1, weights) + 0.04 * heat_noise)[0]
    center = jnp.asarray([0.045, 0.08, 0.016, 0.016, 0.2, 0.0125, 0.016, 0.016, 0.55], jnp.float32).reshape(9, 1, 1, 1)
    amplitude = jnp.asarray([0.015, 0.02, 0.004, 0.004, 0.1, 0.0015, 0.004, 0.004, 0.1], jnp.float32).reshape(9, 1, 1, 1)
    width = jnp.asarray([0.005, 0.005, 0.001, 0.001, 0.05, 0.0005, 0.001, 0.001, 0.03], jnp.float32).reshape(9, 1, 1, 1)
    fractions = center + amplitude * wave_stack(keys[9], 9, weights) + width * species_noise
    kinetic = 0.5 * (velocity[0] * velocity[0] + velocity[1] * velocity[1] + velocity[2] * velocity[2])
    energy = density * (internal + kinetic)
    species = density * fractions
    return jnp.concatenate([density[None], density * velocity, energy[None], species], axis=0).astype(jnp.float32)


def block_levels(stream_key, shape, shards, smallest, largest):
    level, own = 1.0, jax.random.fold_in(stream_key, 6)
    for axis_at, blocks in shards:
        steps = jnp.exp(jax.random.uniform(jax.random.fold_in(own, axis_at), (blocks,), jnp.float32, smallest / len(shards), largest / len(shards)))
        level = level * jnp.repeat(steps, shape[axis_at] // blocks).reshape([-1 if axis == axis_at else 1 for axis in range(len(shape))])
    return level


def setup_inputs(seed: int = 0) -> dict:
    splits = jax.random.split(jax.random.key(seed), 3)
    fields = draw_fields(jax.random.fold_in(splits[2], 71), 0)
    register = jnp.clip(jax.random.uniform(splits[1], (FIELDS, Z, NX, NY), jnp.float32, -0.15, 0.15) * block_levels(splits[1], (FIELDS, Z, NX, NY), ((2, 8), (3, 4)), -0.4, 0.0), -0.15, 0.15)
    return dict(fields=fields, register=register)


GAMMA_LESS = 0.4
UNIVERSAL_R = 0.25
TIME_STEP = 0.25
SECTION_DECAY = -0.4178904745
SECTION_WEIGHT = 0.3792103129
GRAD_FLOOR = 0.1
PROGRESS_SCALE = 4.0
CENTRAL_WEIGHTS = (0.8, -0.2, 4.0 / 105.0, -1.0 / 280.0)
MOLAR_MASS = (2.0, 32.0, 16.0, 17.0, 18.0, 1.0, 33.0, 34.0, 28.0)
FORMATION_HEAT = (0.0, 0.0, 2.0, 0.3, -1.5, 3.0, 0.1, -0.4, 0.0)
ARRHENIUS_LIST = ((5, 1, (2, 3), 40.0, 2.0), (2, 0, (5, 3), 30.0, 1.2), (3, 0, (5, 4), 25.0, 0.8), (2, 4, (3, 3), 10.0, 1.6), (5, 1, (6,), 15.0, 0.2), (6, 5, (3, 3), 20.0, 0.3), (6, 6, (7, 1), 12.0, 0.4), (7, 8, (3, 3, 8), 8.0, 1.8))

def make_table():
    table = np.zeros((14, 8))
    for column, kinetic_step_record in enumerate(ARRHENIUS_LIST):
        change = np.zeros(9)
        change[kinetic_step_record[0]] -= 1.0
        change[kinetic_step_record[1]] -= 1.0
        for product in kinetic_step_record[2]:
            change[product] += 1.0
        for species in range(9):
            mass_change = MOLAR_MASS[species] / 18.0 * change[species]
            table[5 + species, column] = mass_change
            table[4, column] -= FORMATION_HEAT[species] * mass_change
    return table

def inverse_weights():
    return np.array([18.0 / value for value in MOLAR_MASS])

def primitives(fields):
    velocity = fields[1:4] / fields[0]
    static_stress = GAMMA_LESS * (fields[4] - 0.5 * (fields[1] * velocity[0] + fields[2] * velocity[1] + fields[3] * velocity[2]))
    return (velocity, static_stress)

def reaction_rates(fields, static_stress):
    species_quantities = fields[5:14] * jnp.asarray(inverse_weights(), jnp.float32).reshape(9, 1, 1, 1)
    summed_quantity = lax.optimization_barrier(jnp.sum(species_quantities, axis=0))
    cell_thermal_state = static_stress / (UNIVERSAL_R * summed_quantity)
    return jnp.stack([kinetic_step_record[3] * jnp.exp(-kinetic_step_record[4] / cell_thermal_state) * species_quantities[kinetic_step_record[0]] * species_quantities[kinetic_step_record[1]] for kinetic_step_record in ARRHENIUS_LIST])

def rolled_central(values, along):
    total = jnp.zeros_like(values)
    for offset, weight in enumerate(CENTRAL_WEIGHTS, 1):
        total = total + weight * (jnp.roll(values, -offset, along) - jnp.roll(values, offset, along))
    return total

def flame_metrics(padded):
    scalar = padded[0]
    grad_z = (scalar[2:, 1:-1, 1:-1] - scalar[:-2, 1:-1, 1:-1]) * 0.5
    grad_x = (scalar[1:-1, 2:, 1:-1] - scalar[1:-1, :-2, 1:-1]) * 0.5
    grad_y = (scalar[1:-1, 1:-1, 2:] - scalar[1:-1, 1:-1, :-2]) * 0.5
    magnitude = jnp.maximum(jnp.sqrt(grad_x * grad_x + grad_y * grad_y + grad_z * grad_z), GRAD_FLOOR)
    normal_x = -grad_x / magnitude
    normal_y = -grad_y / magnitude
    normal_z = -grad_z / magnitude
    curvature = 0.5 * (normal_x[1:-1, 2:, 1:-1] - normal_x[1:-1, :-2, 1:-1])
    curvature = curvature + 0.5 * (normal_y[1:-1, 1:-1, 2:] - normal_y[1:-1, 1:-1, :-2])
    curvature = curvature + 0.5 * (normal_z[2:, 1:-1, 1:-1] - normal_z[:-2, 1:-1, 1:-1])
    inner = (normal_x[1:-1, 1:-1, 1:-1], normal_y[1:-1, 1:-1, 1:-1], normal_z[1:-1, 1:-1, 1:-1])
    speeds = padded[1:4]
    gradients = []
    for component in range(3):
        piece = speeds[component]
        along_x = (piece[2:-2, 3:-1, 2:-2] - piece[2:-2, 1:-3, 2:-2]) * 0.5
        along_y = (piece[2:-2, 2:-2, 3:-1] - piece[2:-2, 2:-2, 1:-3]) * 0.5
        along_z = (piece[3:-1, 2:-2, 2:-2] - piece[1:-3, 2:-2, 2:-2]) * 0.5
        gradients.append((along_x, along_y, along_z))
    strain = gradients[0][0] + gradients[1][1] + gradients[2][2]
    for component in range(3):
        for direction in range(3):
            strain = strain - inner[component] * inner[direction] * gradients[component][direction]
    return jnp.stack([inner[0], inner[1], inner[2], curvature, strain])

def reference(fields, register):
    velocity, static_stress = primitives(fields)
    rates = reaction_rates(fields, static_stress)
    chem = jnp.asarray(make_table(), jnp.float32)

    def per_field(item):
        index, values, stored = item
        source = jnp.tensordot(chem[index], rates, axes=1, precision=lax.Precision.HIGHEST)
        advection = jnp.zeros_like(values)
        for direction, along in ((0, 1), (1, 2), (2, 0)):
            is_moment = (index == 1 + direction).astype(jnp.float32)
            is_energy = (index == 4).astype(jnp.float32)
            flux = values * velocity[direction] + static_stress * is_moment + static_stress * velocity[direction] * is_energy
            advection = advection + rolled_central(flux, along)
        stored_next = SECTION_DECAY * stored + TIME_STEP * (source - advection)
        return (values + SECTION_WEIGHT * stored_next, stored_next)
    indices = jnp.arange(fields.shape[0], dtype=jnp.int32)
    fields_next, register_next = lax.map(per_field, (indices, fields, register))
    probe = jnp.stack([PROGRESS_SCALE * (fields[9] / fields[0]), velocity[0], velocity[1], velocity[2]]).astype(jnp.bfloat16)
    padded = jnp.pad(probe.astype(jnp.float32), ((0, 0), (2, 2), (2, 2), (2, 2)), mode='wrap')
    metrics = flame_metrics(padded).astype(jnp.bfloat16)
    return (fields_next, register_next, metrics)
```

```python
import functools

import jax
import jax.numpy as jnp
import numpy as np
from jax import lax
from jax.experimental import pallas as pl
from jax.experimental.pallas import tpu as pltpu
from jax.sharding import PartitionSpec as P

GAMMA_LESS = 0.4
UNIVERSAL_R = 0.25
TIME_STEP = 0.25
SECTION_DECAY = -0.4178904745
SECTION_WEIGHT = 0.3792103129
GRAD_FLOOR = 0.1
PROGRESS_SCALE = 4.0
CENTRAL_WEIGHTS = (0.8, -0.2, 4.0 / 105.0, -1.0 / 280.0)
WHOLE_WEIGHTS = (672.0, -168.0, 32.0, -3.0)
WHOLE_SCALE = 1.0 / 840.0
MOLAR_MASS = (2.0, 32.0, 16.0, 17.0, 18.0, 1.0, 33.0, 34.0, 28.0)
FORMATION_HEAT = (0.0, 0.0, 2.0, 0.3, -1.5, 3.0, 0.1, -0.4, 0.0)
ARRHENIUS_LIST = (
    (5, 1, (2, 3), 40.0, 2.0),
    (2, 0, (5, 3), 30.0, 1.2),
    (3, 0, (5, 4), 25.0, 0.8),
    (2, 4, (3, 3), 10.0, 1.6),
    (5, 1, (6,), 15.0, 0.2),
    (6, 5, (3, 3), 20.0, 0.3),
    (6, 6, (7, 1), 12.0, 0.4),
    (7, 8, (3, 3, 8), 8.0, 1.8),
)
FIELDS = 14
FLOWS = 5
LAYERS = 4 * FIELDS + FLOWS
MIB = 1 << 20
F32 = jnp.float32
BF16 = jnp.bfloat16


def make_table():
    table = np.zeros((14, 8))
    for column, step in enumerate(ARRHENIUS_LIST):
        change = np.zeros(9)
        change[step[0]] -= 1.0
        change[step[1]] -= 1.0
        for product in step[2]:
            change[product] += 1.0
        for species in range(9):
            mass_change = MOLAR_MASS[species] / 18.0 * change[species]
            table[5 + species, column] = mass_change
            table[4, column] -= FORMATION_HEAT[species] * mass_change
    return table


def ring(axis):
    count = lax.axis_size(axis)
    forward = [(i, (i + 1) % count) for i in range(count)]
    backward = [(target, source) for source, target in forward]
    return forward, backward


def lane_cell(lane):
    place = lane % 64
    return place % 4 if place < 4 * FIELDS else 0


def face_matrix():
    weights = np.zeros((128, 128), np.float32)
    for lane in range(64):
        cell = lane_cell(lane)
        for k in range(4 - cell):
            weights[k, lane] = WHOLE_WEIGHTS[k + cell]
            weights[127 - k, 64 + lane] = -WHOLE_WEIGHTS[k + cell]
    return np.concatenate([weights, weights], axis=0)


def place_matrix():
    weights = np.zeros((128, 128), np.float32)
    for lane in range(64):
        cell = lane_cell(lane)
        weights[lane, 127 - cell] = 1.0
        weights[64 + lane, cell] = 1.0
    return weights


def line_matrix():
    weights = np.zeros((128, 128), np.float32)
    for out in range(128):
        for m in range(1, 5):
            if out + m < 128:
                weights[out + m, out] = WHOLE_WEIGHTS[m - 1]
            if out - m >= 0:
                weights[out - m, out] = -WHOLE_WEIGHTS[m - 1]
    return np.concatenate([weights, weights], axis=0)


def lane_mask(field):
    lanes = lax.broadcasted_iota(jnp.int32, (1, 128), 1) % 64
    mask = (lanes >= 4 * field) & (lanes < 4 * field + 4)
    if field < FLOWS:
        mask = mask | (lanes == 4 * FIELDS + field)
    return mask


def two_terms(value):
    high = value.astype(BF16)
    low = (value - high.astype(F32)).astype(BF16)
    return high, low


def in_vmem(count):
    return [pl.BlockSpec(memory_space=pltpu.VMEM)] * count


def in_hbm(count):
    return [pl.BlockSpec(memory_space=pltpu.HBM)] * count


def wrapped(start, size, depth):
    pieces = []
    at = start
    while at < start + size:
        inside = at % depth
        length = min(start + size - at, depth - inside)
        pieces.append(((at - start) * 16, length * 16, inside * 16))
        at += length
    return pieces


def front_kernel(
    count, fields_ref, flat, prim, main_ref, low_edge_ref, high_edge_ref, low_ref, high_ref, progress, edge, arrived
):
    rows = flat.shape[1]
    depth = rows // 16
    own = depth // count
    chunk = 256

    def arrival(step):
        there = pl.ds(pl.multiple_of(step * chunk, chunk), chunk)
        return pltpu.make_async_copy(
            fields_ref.at[:, there, :], flat.at[:, there, :], arrived.at[step]
        )

    for step in range(rows // chunk):
        arrival(step).start()

    def chunk_body(step, carry):
        arrival(step).wait()

        def fill(part, inner_carry):
            at = pl.ds(pl.multiple_of(step * chunk + part * 64, 64), 64)
            density = flat[0, at, :]
            mx, my, mz, energy = [flat[c, at, :] for c in range(1, 5)]
            u, v, w = mx / density, my / density, mz / density
            stress = GAMMA_LESS * (energy - 0.5 * (mx * u + my * v + mz * w))
            progress[at, :] = PROGRESS_SCALE * (flat[9, at, :] / density)
            prim[0, at, :] = u
            prim[1, at, :] = v
            prim[2, at, :] = w
            prim[3, at, :] = stress
            flat[4, at, :] = energy + stress
            return inner_carry

        lax.fori_loop(0, chunk // 64, fill, 0)
        planes = pl.ds(pl.multiple_of(step * 16, 16), 16)

        def layer(ref, index, x):
            return ref[index, pl.ds(step * chunk + x, 16, stride=16), :]

        for ref, layers, sign in ((low_ref, (0, 1, 2, 3), 1.0), (high_ref, (15, 14, 13, 12), -1.0)):
            speeds = [layer(prim, 0, x) for x in layers]
            for field in range(FIELDS):
                flux = [layer(flat, field, x) * speeds[k] for k, x in enumerate(layers)]
                if field == 1:
                    flux = [flux[k] + layer(prim, 3, x) for k, x in enumerate(layers)]
                for cell in range(4):
                    part = (sign * CENTRAL_WEIGHTS[cell]) * flux[0]
                    for k in range(1, 4 - cell):
                        part = part + (sign * CENTRAL_WEIGHTS[k + cell]) * flux[k]
                    high, low = two_terms(part)
                    ref[4 * field + cell, planes, :] = high
                    if cell == 0 and field < FLOWS:
                        ref[4 * FIELDS + field, planes, :] = low
        return carry

    lax.fori_loop(0, rows // chunk, chunk_body, 0)

    edge[...] = jnp.zeros(edge.shape, F32)
    for j in range(count):
        offset = 0
        for c in range(4):
            margin = 2 if c == 0 else 1
            for to, length, source in wrapped(own * j - margin, own + 2 * margin, depth):
                piece = progress[source : source + length, :] if c == 0 else prim[c - 1, source : source + length, :]
                main_ref[j, offset + to : offset + to + length, :] = piece.astype(BF16)
            offset += (own + 2 * margin) * 16
        for ref, first, second in ((low_edge_ref, 0, 1), (high_edge_ref, 15, 14)):
            for to, length, source in wrapped(own * j - 1, own + 2, depth):
                edge[to // 16 : (to + length) // 16, :] = progress[pl.ds(source + first, length // 16, stride=16), :]
            edge[own + 2 : 2 * own + 2, :] = progress[pl.ds(own * j * 16 + second, own, stride=16), :]
            for c in range(3):
                start = (c + 2) * own + 2
                edge[start : start + own, :] = prim[c, pl.ds(own * j * 16 + first, own, stride=16), :]
            ref[j, :, :] = edge[...].astype(BF16)


def front_part(fields, count):
    rows = fields.shape[1]
    depth = rows // 16
    own = depth // count
    main_rows = (4 * own + 10) * 16
    edge_rows = -(-(5 * own + 2) // 16) * 16
    return pl.pallas_call(
        functools.partial(front_kernel, count),
        in_specs=in_hbm(1),
        out_specs=in_vmem(7),
        out_shape=[
            jax.ShapeDtypeStruct((FIELDS, rows, 128), F32),
            jax.ShapeDtypeStruct((4, rows, 128), F32),
            jax.ShapeDtypeStruct((count, main_rows, 128), BF16),
            jax.ShapeDtypeStruct((count, edge_rows, 128), BF16),
            jax.ShapeDtypeStruct((count, edge_rows, 128), BF16),
            jax.ShapeDtypeStruct((LAYERS, depth, 128), BF16),
            jax.ShapeDtypeStruct((LAYERS, depth, 128), BF16),
        ],
        scratch_shapes=[
            pltpu.VMEM((rows, 128), F32),
            pltpu.VMEM((edge_rows, 128), F32),
            pltpu.SemaphoreType.DMA((rows // 256,)),
        ],
        compiler_params=pltpu.CompilerParams(vmem_limit_bytes=40 * MIB),
        cost_estimate=pl.CostEstimate(flops=100 * rows * 128, bytes_accessed=10 * MIB, transcendentals=0),
        name="front_part",
    )(fields)


def lines_kernel(flat, prim, weights_ref, terms, low_ref, high_ref, total):
    rows = flat.shape[1]
    half = rows // 2

    def fill(step, carry):
        at = pl.ds(pl.multiple_of(step * 32, 32), 32)
        v = prim[1, at, :]
        for field in range(FIELDS):
            flux = flat[field, at, :] * v
            if field == 2:
                flux = flux + prim[3, at, :]
            high, low = two_terms(flux)
            terms[field, at, 0:128] = high
            terms[field, at, 128:256] = low
        return carry

    lax.fori_loop(0, rows // 32, fill, 0)
    weights = weights_ref[...]
    for field in range(FIELDS):
        product = jnp.dot(terms[field], weights, preferred_element_type=F32)
        if field == 0:
            total[...] = product
        else:
            total[...] = jnp.where(lane_mask(field), product, total[...])
    value = total[...] * WHOLE_SCALE
    lanes = lax.broadcasted_iota(jnp.int32, (1, 128), 1)
    second = lanes % 64 >= 4 * FIELDS
    value = jnp.where(second, value - value.astype(BF16).astype(F32), value)
    turned = pltpu.roll(value, 64, 1)
    low_ref[...] = jnp.where(lanes < 64, value[0:half, :], turned[half:rows, :]).astype(BF16)
    high_ref[...] = jnp.where(lanes < 64, turned[0:half, :], value[half:rows, :]).astype(BF16)


def lines_part(flat, prim):
    rows = flat.shape[1]
    return pl.pallas_call(
        lines_kernel,
        in_specs=in_vmem(3),
        out_specs=in_vmem(3),
        out_shape=[
            jax.ShapeDtypeStruct((FIELDS, rows, 256), BF16),
            jax.ShapeDtypeStruct((rows // 2, 128), BF16),
            jax.ShapeDtypeStruct((rows // 2, 128), BF16),
        ],
        scratch_shapes=[pltpu.VMEM((rows, 128), F32)],
        compiler_params=pltpu.CompilerParams(vmem_limit_bytes=40 * MIB),
        cost_estimate=pl.CostEstimate(flops=300 * rows * 128, bytes_accessed=8 * MIB, transcendentals=0),
        name="lines_part",
    )(flat, prim, jnp.asarray(face_matrix(), BF16))


def sources(species, stress):
    moles = [species[k] * (18.0 / MOLAR_MASS[k]) for k in range(9)]
    summed = moles[0]
    for k in range(1, 9):
        summed = summed + moles[k]
    inverse_heat = UNIVERSAL_R * summed / stress
    e02 = jnp.exp(-0.2 * inverse_heat)
    e03 = jnp.exp(-0.3 * inverse_heat)
    e04 = e02 * e02
    e08 = e04 * e04
    e16 = e08 * e08
    powers = {0.2: e02, 0.3: e03, 0.4: e04, 0.8: e08, 1.6: e16}
    powers[1.2] = e08 * e04
    powers[1.8] = e16 * e02
    powers[2.0] = e16 * e04
    rates = [
        (step[3] * powers[step[4]]) * (moles[step[0]] * moles[step[1]]) for step in ARRHENIUS_LIST
    ]
    table = make_table()
    result = []
    for field in range(FIELDS):
        value = None
        for column in range(8):
            factor = float(table[field, column])
            if factor != 0.0:
                term = (TIME_STEP * factor) * rates[column]
                value = term if value is None else value + term
        result.append(value)
    return result


def windowed(flux, first, planes):
    window = {z: flux(z) for z in range(first - 4, first + 4)}
    for z in range(first, first + planes):
        window[z + 4] = flux(z + 4)
        change = None
        for m, weight in enumerate(CENTRAL_WEIGHTS, 1):
            term = (-TIME_STEP * weight) * (window[z + m] - window[z - m])
            change = term if change is None else change + term
        yield z, change


def inner_kernel(flat, prim, register, terms, line_ref, out, flux_x, along_y):
    rows = flat.shape[1]
    depth = rows // 16
    flux_x[:, 0:8, :] = jnp.zeros((depth, 8, 128), F32)
    flux_x[:, 24:32, :] = jnp.zeros((depth, 8, 128), F32)

    def react(step, carry):
        at = pl.ds(pl.multiple_of(step * 32, 32), 32)
        made = sources([flat[5 + k, at, :] for k in range(9)], prim[3, at, :])
        for field in range(FIELDS):
            kept = SECTION_DECAY * register[field, at, :]
            out[field, at, :] = kept if made[field] is None else kept + made[field]
        return carry

    lax.fori_loop(0, rows // 32, react, 0)

    def spread(field, flux, extra):
        for z in range(depth):
            flux_x[z, 8:24, :] = flux(0, z * 16, 16)
        for first in range(0, depth, 16):
            for tile in range(2):
                row = 8 * tile
                for z, change in windowed(lambda z: flux(2, (z % depth) * 16 + row, 8), first, 16):
                    for m, weight in enumerate(CENTRAL_WEIGHTS, 1):
                        at = 8 + row
                        change = change + (-TIME_STEP * weight) * (
                            flux_x[z, at + m : at + m + 8, :] - flux_x[z, at - m : at - m + 8, :]
                        )
                    extra(z * 16 + row, change)

    def across(field, carry):
        along_y[...] = jnp.dot(terms[field], line_ref[...], preferred_element_type=F32)

        def flux(direction, row, size):
            return flat[field, row : row + size, :] * prim[direction, row : row + size, :]

        def extra(row, change):
            at = slice(row, row + 8)
            out[field, at, :] += change + (-TIME_STEP * WHOLE_SCALE) * along_y[at, :]

        spread(field, flux, extra)
        return carry

    lax.fori_loop(0, FIELDS, across, 0)

    for z in range(depth):
        flux_x[z, 8:24, :] = prim[3, z * 16 : z * 16 + 16, :]
    for first in range(0, depth, 16):
        for tile in range(2):
            row = 8 * tile

            def stress(z):
                at = (z % depth) * 16 + row
                return prim[3, at : at + 8, :]

            for z, change in windowed(stress, first, 16):
                at = slice(z * 16 + row, z * 16 + row + 8)
                out[3, at, :] += change
                change = None
                for m, weight in enumerate(CENTRAL_WEIGHTS, 1):
                    low = 8 + row
                    term = (-TIME_STEP * weight) * (
                        flux_x[z, low + m : low + m + 8, :] - flux_x[z, low - m : low - m + 8, :]
                    )
                    change = term if change is None else change + term
                out[1, at, :] += change


def inner_part(flat, prim, register, terms):
    rows = flat.shape[1]
    depth = rows // 16
    return pl.pallas_call(
        inner_kernel,
        in_specs=in_vmem(5),
        out_specs=pl.BlockSpec(memory_space=pltpu.VMEM),
        out_shape=jax.ShapeDtypeStruct((FIELDS, rows, 128), F32),
        scratch_shapes=[
            pltpu.VMEM((depth, 32, 128), F32),
            pltpu.VMEM((rows, 128), F32),
        ],
        compiler_params=pltpu.CompilerParams(vmem_limit_bytes=40 * MIB),
        cost_estimate=pl.CostEstimate(
            flops=2000 * rows * 128, bytes_accessed=20 * MIB, transcendentals=10 * rows * 128
        ),
        name="inner_part",
    )(flat, prim, register, terms, jnp.asarray(line_matrix(), BF16))


def outer_kernel(
    part, flat, prim, prev, following, yprev, ynext, place_ref, fields_out, register_out,
    faces_x, along_y, message, fields_stage, register_stage, sent,
):
    rows = part.shape[1]
    depth = rows // 16
    half = rows // 2
    lanes = lax.broadcasted_iota(jnp.int32, (1, 128), 1)
    low = ynext[...].astype(F32)
    high = yprev[...].astype(F32)
    message[0:half, :] = jnp.where(lanes < 64, low, pltpu.roll(high, 64, 1)).astype(BF16)
    message[half:rows, :] = jnp.where(lanes < 64, pltpu.roll(low, 64, 1), high).astype(BF16)
    faces_x[...] = jnp.zeros(faces_x.shape, F32)
    place = place_ref[...]
    copies = []
    for field in range(FIELDS):
        for ref, layers in ((prev, (0, 1, 2, 3)), (following, (15, 14, 13, 12))):
            for cell, x in enumerate(layers):
                value = ref[4 * field + cell, :, :].astype(F32)
                if cell == 0 and field < FLOWS:
                    value = value + ref[4 * FIELDS + field, :, :].astype(F32)
                faces_x[pl.ds(x, depth, stride=16), :] = value
        held = message[...]
        picked = jnp.where(lane_mask(field), held, jnp.zeros_like(held))
        along_y[...] = jnp.dot(picked, place, preferred_element_type=F32)
        stored = part[field] - TIME_STEP * (along_y[...] + faces_x[...])
        register_stage[field] = stored
        before = flat[field]
        if field == 4:
            before = before - prim[3]
        fields_stage[field] = before + SECTION_WEIGHT * stored
        for index, (stage, ref) in enumerate(((register_stage, register_out), (fields_stage, fields_out))):
            copy = pltpu.make_async_copy(stage.at[field], ref.at[field], sent.at[index, field])
            copy.start()
            copies.append(copy)
    for copy in copies:
        copy.wait()


def outer_part(part, flat, prim, prev, following, yprev, ynext):
    rows = flat.shape[1]
    return pl.pallas_call(
        outer_kernel,
        in_specs=in_vmem(8),
        out_specs=in_hbm(2),
        out_shape=[jax.ShapeDtypeStruct((FIELDS, rows, 128), F32)] * 2,
        scratch_shapes=[
            pltpu.VMEM((rows, 128), F32),
            pltpu.VMEM((rows, 128), F32),
            pltpu.VMEM((rows, 128), BF16),
            pltpu.VMEM((FIELDS, rows, 128), F32),
            pltpu.VMEM((FIELDS, rows, 128), F32),
            pltpu.SemaphoreType.DMA((2, FIELDS)),
        ],
        compiler_params=pltpu.CompilerParams(vmem_limit_bytes=40 * MIB),
        cost_estimate=pl.CostEstimate(
            flops=100 * rows * 128, bytes_accessed=24 * MIB, transcendentals=0
        ),
        name="outer_part",
    )(part, flat, prim, prev, following, yprev, ynext, jnp.asarray(place_matrix(), BF16))


def lane_difference(values):
    lanes = lax.broadcasted_iota(jnp.int32, values[0].shape, 1)
    ahead = [pltpu.roll(value, 127, 1) for value in values]
    behind = [pltpu.roll(value, 1, 1) for value in values]
    count = len(values)
    return [
        jnp.where(lanes == 127, ahead[(j + 1) % count], ahead[j])
        - jnp.where(lanes == 0, behind[(j - 1) % count], behind[j])
        for j in range(count)
    ]


def inverse_length(a, b, c):
    return 1.0 * lax.rsqrt(jnp.maximum(a * a + b * b + c * c, GRAD_FLOOR * GRAD_FLOOR))


def metrics_kernel(count, own, blocks, out_ref, scalar, speed, normal, normal_z, edge, stage, sent):
    start_edge = (4 * own + 10) * 16
    half = (blocks.shape[1] - start_edge) // 2
    edge[...] = blocks[:, start_edge:, :].astype(F32)
    for j in range(count):
        for z in range(own + 4):
            scalar[j, pl.ds(z * 32 + 8, 16), :] = blocks[j, z * 16 : z * 16 + 16, :].astype(F32)
        for c in range(3):
            base = (own + 4 + c * (own + 2)) * 16
            for z in range(own + 2):
                speed[c, j, pl.ds(z * 32 + 8, 16), :] = blocks[
                    j, base + z * 16 : base + z * 16 + 16, :
                ].astype(F32)
        for side, row in ((0, 7), (half, 24)):
            scalar[j, pl.ds(32 + row, own + 2, stride=32), :] = edge[j, side : side + own + 2, :]
            for c in range(3):
                start = side + (c + 2) * own + 2
                speed[c, j, pl.ds(32 + row, own, stride=32), :] = edge[j, start : start + own, :]

    for side, inside, row in ((0, 8, 7), (half, 23, 24)):
        sign = 0.5 if row == 7 else -0.5
        lines = [edge[j, side + 1 : side + 1 + own, :] for j in range(count)]
        along_y = lane_difference(lines)
        for j in range(count):
            beyond = edge[j, side + own + 2 : side + 2 * own + 2, :]
            grad_x = sign * (scalar[j, pl.ds(64 + inside, own, stride=32), :] - beyond)
            grad_y = 0.5 * along_y[j]
            grad_z = 0.5 * (edge[j, side + 2 : side + 2 + own, :] - edge[j, side : side + own, :])
            normal[0, j, pl.ds(32 + row, own, stride=32), :] = -grad_x * inverse_length(
                grad_x, grad_y, grad_z
            )

    def window(z, row):
        return pl.ds(pl.multiple_of(z * 32, 32) + row, 16)

    def find_normals(z, carry):
        along_y = lane_difference([scalar[j, window(z + 1, 8), :] for j in range(count)])
        for j in range(count):
            grad_x = 0.5 * (scalar[j, window(z + 1, 9), :] - scalar[j, window(z + 1, 7), :])
            grad_y = 0.5 * along_y[j]
            grad_z = 0.5 * (scalar[j, window(z + 2, 8), :] - scalar[j, window(z, 8), :])
            scale = -inverse_length(grad_x, grad_y, grad_z)
            normal[0, j, window(z, 8), :] = grad_x * scale
            normal[1, j, window(z, 8), :] = grad_y * scale
            normal_z[j, z, :, :] = grad_z * scale
        return carry

    lax.fori_loop(0, own + 2, find_normals, 0)

    def find_metrics(z, carry):
        curve_y = lane_difference([normal[1, j, window(z + 1, 8), :] for j in range(count)])
        speed_y = [
            lane_difference([speed[c, j, window(z + 1, 8), :] for j in range(count)])
            for c in range(3)
        ]
        for j in range(count):
            lanes = slice(j * 128, j * 128 + 128)
            normals = [
                normal[0, j, window(z + 1, 8), :],
                normal[1, j, window(z + 1, 8), :],
                normal_z[j, z + 1, :, :],
            ]
            curvature = 0.5 * (
                (normal[0, j, window(z + 1, 9), :] - normal[0, j, window(z + 1, 7), :])
                + curve_y[j]
                + (normal_z[j, z + 2, :, :] - normal_z[j, z, :, :])
            )
            strain = None
            for c in range(3):
                slopes = [
                    speed[c, j, window(z + 1, 9), :] - speed[c, j, window(z + 1, 7), :],
                    speed_y[c][j],
                    speed[c, j, window(z + 2, 8), :] - speed[c, j, window(z, 8), :],
                ]
                along = normals[0] * slopes[0] + normals[1] * slopes[1] + normals[2] * slopes[2]
                term = slopes[c] - normals[c] * along
                strain = term if strain is None else strain + term
            for index, value in enumerate(normals + [curvature, 0.5 * strain]):
                stage[index, z, :, lanes] = value.astype(BF16)
        pltpu.make_async_copy(stage.at[:, z], out_ref.at[:, z], sent.at[z]).start()
        return carry

    lax.fori_loop(0, own, find_metrics, 0)
    for z in range(own):
        pltpu.make_async_copy(stage.at[:, z], out_ref.at[:, z], sent.at[z]).wait()


def metrics_part(blocks, own):
    count = blocks.shape[0]
    half = (blocks.shape[1] - (4 * own + 10) * 16) // 2
    shape = (5, own, 16, count * 128)
    return pl.pallas_call(
        functools.partial(metrics_kernel, count, own),
        in_specs=in_vmem(1),
        out_specs=in_hbm(1)[0],
        out_shape=jax.ShapeDtypeStruct(shape, BF16),
        scratch_shapes=[
            pltpu.VMEM((count, (own + 4) * 32, 128), F32),
            pltpu.VMEM((3, count, (own + 2) * 32, 128), F32),
            pltpu.VMEM((2, count, (own + 2) * 32, 128), F32),
            pltpu.VMEM((count, own + 2, 16, 128), F32),
            pltpu.VMEM((count, 2 * half, 128), F32),
            pltpu.VMEM(shape, BF16),
            pltpu.SemaphoreType.DMA((own,)),
        ],
        compiler_params=pltpu.CompilerParams(vmem_limit_bytes=40 * MIB),
        cost_estimate=pl.CostEstimate(
            flops=300 * own * 16 * 128 * count, bytes_accessed=3 * MIB, transcendentals=0
        ),
        name="flame_metrics",
    )(blocks)


def per_device(fields, register):
    depth, count_x, count_y = fields.shape[1:]
    flat = fields.reshape(FIELDS, depth * count_x, count_y)
    count = lax.axis_size("gy")
    own = depth // count
    x_forward, x_backward = ring("gx")
    y_forward, y_backward = ring("gy")

    flat, prim, main, edge_low, edge_high, low, high = front_part(flat, count)
    edge_prev = lax.ppermute(edge_high, "gx", x_forward)
    edge_next = lax.ppermute(edge_low, "gx", x_backward)
    following = lax.ppermute(low, "gx", x_backward)
    prev = lax.ppermute(high, "gx", x_forward)
    terms, ylow, yhigh = lines_part(flat, prim)
    blocks = lax.all_to_all(
        jnp.concatenate([main, edge_prev, edge_next], axis=1), "gy", 0, 0, tiled=True
    )
    ynext = lax.ppermute(ylow, "gy", y_backward)
    yprev = lax.ppermute(yhigh, "gy", y_forward)
    part = inner_part(flat, prim, register.reshape(flat.shape), terms)
    fields_next, register_next = outer_part(part, flat, prim, prev, following, yprev, ynext)
    metrics = metrics_part(blocks, own)
    return (fields_next.reshape(fields.shape), register_next.reshape(fields.shape), metrics)


def solution(mesh):
    in_specs = (P(None, None, "gx", "gy"), P(None, None, "gx", "gy"))
    out_specs = (P(None, None, "gx", "gy"), P(None, None, "gx", "gy"), P(None, "gy", "gx", None))
    return jax.shard_map(
        per_device, mesh=mesh, in_specs=in_specs, out_specs=out_specs, check_vma=False
    )
```

```python
import functools

import jax
import jax.numpy as jnp
import numpy as np
from jax import lax
from jax.experimental import pallas as pl
from jax.experimental.pallas import tpu as pltpu
from jax.sharding import PartitionSpec as P

GAMMA_LESS = 0.4
UNIVERSAL_R = 0.25
TIME_STEP = 0.25
SECTION_DECAY = -0.4178904745
SECTION_WEIGHT = 0.3792103129
GRAD_FLOOR = 0.1
PROGRESS_SCALE = 4.0
CENTRAL_WEIGHTS = (0.8, -0.2, 4.0 / 105.0, -1.0 / 280.0)
WHOLE_WEIGHTS = (672.0, -168.0, 32.0, -3.0)
WHOLE_SCALE = 1.0 / 840.0
MOLAR_MASS = (2.0, 32.0, 16.0, 17.0, 18.0, 1.0, 33.0, 34.0, 28.0)
FORMATION_HEAT = (0.0, 0.0, 2.0, 0.3, -1.5, 3.0, 0.1, -0.4, 0.0)
ARRHENIUS_LIST = (
    (5, 1, (2, 3), 40.0, 2.0),
    (2, 0, (5, 3), 30.0, 1.2),
    (3, 0, (5, 4), 25.0, 0.8),
    (2, 4, (3, 3), 10.0, 1.6),
    (5, 1, (6,), 15.0, 0.2),
    (6, 5, (3, 3), 20.0, 0.3),
    (6, 6, (7, 1), 12.0, 0.4),
    (7, 8, (3, 3, 8), 8.0, 1.8),
)
FIELDS = 14
FLOWS = 5
LAYERS = 4 * FIELDS + FLOWS
MIB = 1 << 20
F32 = jnp.float32
BF16 = jnp.bfloat16


def make_table():
    table = np.zeros((14, 8))
    for column, step in enumerate(ARRHENIUS_LIST):
        change = np.zeros(9)
        change[step[0]] -= 1.0
        change[step[1]] -= 1.0
        for product in step[2]:
            change[product] += 1.0
        for species in range(9):
            mass_change = MOLAR_MASS[species] / 18.0 * change[species]
            table[5 + species, column] = mass_change
            table[4, column] -= FORMATION_HEAT[species] * mass_change
    return table


def ring(axis):
    count = lax.axis_size(axis)
    forward = [(i, (i + 1) % count) for i in range(count)]
    backward = [(target, source) for source, target in forward]
    return forward, backward


def lane_cell(lane):
    place = lane % 64
    return place % 4 if place < 4 * FIELDS else 0


def face_matrix():
    weights = np.zeros((128, 128), np.float32)
    for lane in range(64):
        cell = lane_cell(lane)
        for k in range(4 - cell):
            weights[k, lane] = WHOLE_WEIGHTS[k + cell]
            weights[127 - k, 64 + lane] = -WHOLE_WEIGHTS[k + cell]
    return np.concatenate([weights, weights], axis=0)


def place_matrix():
    weights = np.zeros((128, 128), np.float32)
    for lane in range(64):
        cell = lane_cell(lane)
        weights[lane, 127 - cell] = 1.0
        weights[64 + lane, cell] = 1.0
    return weights


def line_matrix():
    weights = np.zeros((128, 128), np.float32)
    for out in range(128):
        for m in range(1, 5):
            if out + m < 128:
                weights[out + m, out] = WHOLE_WEIGHTS[m - 1]
            if out - m >= 0:
                weights[out - m, out] = -WHOLE_WEIGHTS[m - 1]
    return np.concatenate([weights, weights], axis=0)


def planes_matrix():
    weights = np.zeros((128, 128), np.float32)
    for out in range(128):
        for m in range(1, 5):
            if out % 16 + m < 16:
                weights[out, out + m] = WHOLE_WEIGHTS[m - 1]
            if out % 16 - m >= 0:
                weights[out, out - m] = -WHOLE_WEIGHTS[m - 1]
    return np.concatenate([weights, weights], axis=1)


def lane_mask(field):
    lanes = lax.broadcasted_iota(jnp.int32, (1, 128), 1) % 64
    mask = (lanes >= 4 * field) & (lanes < 4 * field + 4)
    if field < FLOWS:
        mask = mask | (lanes == 4 * FIELDS + field)
    return mask


def two_terms(value):
    high = value.astype(BF16)
    low = (value - high.astype(F32)).astype(BF16)
    return high, low


def in_vmem(count):
    return [pl.BlockSpec(memory_space=pltpu.VMEM)] * count


def in_hbm(count):
    return [pl.BlockSpec(memory_space=pltpu.HBM)] * count


def wrapped(start, size, depth):
    pieces = []
    at = start
    while at < start + size:
        inside = at % depth
        length = min(start + size - at, depth - inside)
        pieces.append(((at - start) * 16, length * 16, inside * 16))
        at += length
    return pieces


def probe_kernel(count, fields_ref, prim, main_ref, held, progress, arrived):
    rows = prim.shape[1]
    depth = rows // 16
    own = depth // count
    chunk = 256

    def arrival(step):
        there = pl.ds(pl.multiple_of(step * chunk, chunk), chunk)
        return [
            pltpu.make_async_copy(
                fields_ref.at[0:5, there, :], held.at[0:5, there, :], arrived.at[0, step]
            ),
            pltpu.make_async_copy(
                fields_ref.at[9, there, :], held.at[5, there, :], arrived.at[1, step]
            ),
        ]

    for step in range(rows // chunk):
        for copy in arrival(step):
            copy.start()

    def chunk_body(step, carry):
        for copy in arrival(step):
            copy.wait()

        def fill(part, inner_carry):
            at = pl.ds(pl.multiple_of(step * chunk + part * 64, 64), 64)
            density = held[0, at, :]
            mx, my, mz, energy = [held[c, at, :] for c in range(1, 5)]
            u, v, w = mx / density, my / density, mz / density
            stress = GAMMA_LESS * (energy - 0.5 * (mx * u + my * v + mz * w))
            progress[at, :] = PROGRESS_SCALE * (held[5, at, :] / density)
            prim[0, at, :] = u
            prim[1, at, :] = v
            prim[2, at, :] = w
            prim[3, at, :] = stress
            prim[4, at, :] = energy + stress
            return inner_carry

        lax.fori_loop(0, chunk // 64, fill, 0)
        return carry

    lax.fori_loop(0, rows // chunk, chunk_body, 0)

    for j in range(count):
        offset = 0
        for c in range(4):
            margin = 2 if c == 0 else 1
            for to, length, source in wrapped(own * j - margin, own + 2 * margin, depth):
                piece = progress[source : source + length, :] if c == 0 else prim[c - 1, source : source + length, :]
                main_ref[j, offset + to : offset + to + length, :] = piece.astype(BF16)
            offset += (own + 2 * margin) * 16


def probe_part(fields, count):
    rows = fields.shape[1]
    own = rows // 16 // count
    main_rows = (4 * own + 10) * 16
    return pl.pallas_call(
        functools.partial(probe_kernel, count),
        in_specs=in_hbm(1),
        out_specs=in_vmem(2),
        out_shape=[
            jax.ShapeDtypeStruct((5, rows, 128), F32),
            jax.ShapeDtypeStruct((count, main_rows, 128), BF16),
        ],
        scratch_shapes=[
            pltpu.VMEM((6, rows, 128), F32),
            pltpu.VMEM((rows, 128), F32),
            pltpu.SemaphoreType.DMA((2, rows // 256)),
        ],
        compiler_params=pltpu.CompilerParams(vmem_limit_bytes=48 * MIB),
        cost_estimate=pl.CostEstimate(flops=30 * rows * 128, bytes_accessed=5 * MIB, transcendentals=0),
        name="probe_part",
    )(fields)


def faces_kernel(fields_ref, prim, flat, low_ref, high_ref, arrived):
    rows = flat.shape[1]

    def arrival(step):
        there = pl.ds(pl.multiple_of(step * 256, 256), 256)
        return pltpu.make_async_copy(
            fields_ref.at[:, there, :], flat.at[:, there, :], arrived.at[step]
        )

    for step in range(rows // 256):
        arrival(step).start()

    def chunk_body(step, carry):
        arrival(step).wait()
        planes = pl.ds(pl.multiple_of(step * 16, 16), 16)

        def layer(ref, index, x):
            return ref[index, pl.ds(step * 256 + x, 16, stride=16), :]

        for ref, layers, sign in ((low_ref, (0, 1, 2, 3), 1.0), (high_ref, (15, 14, 13, 12), -1.0)):
            speeds = [layer(prim, 0, x) for x in layers]
            for field in range(FIELDS):
                source = (prim, 4) if field == 4 else (flat, field)
                flux = [layer(*source, x) * speeds[k] for k, x in enumerate(layers)]
                if field == 1:
                    flux = [flux[k] + layer(prim, 3, x) for k, x in enumerate(layers)]
                for cell in range(4):
                    part = (sign * CENTRAL_WEIGHTS[cell]) * flux[0]
                    for k in range(1, 4 - cell):
                        part = part + (sign * CENTRAL_WEIGHTS[k + cell]) * flux[k]
                    high, low = two_terms(part)
                    ref[4 * field + cell, planes, :] = high
                    if cell == 0 and field < FLOWS:
                        ref[4 * FIELDS + field, planes, :] = low
        return carry

    lax.fori_loop(0, rows // 256, chunk_body, 0)


def faces_part(fields, prim):
    rows = fields.shape[1]
    depth = rows // 16
    return pl.pallas_call(
        faces_kernel,
        in_specs=in_hbm(1) + in_vmem(1),
        out_specs=in_vmem(3),
        out_shape=[
            jax.ShapeDtypeStruct(fields.shape, F32),
            jax.ShapeDtypeStruct((LAYERS, depth, 128), BF16),
            jax.ShapeDtypeStruct((LAYERS, depth, 128), BF16),
        ],
        scratch_shapes=[pltpu.SemaphoreType.DMA((rows // 256,))],
        compiler_params=pltpu.CompilerParams(vmem_limit_bytes=40 * MIB),
        cost_estimate=pl.CostEstimate(flops=100 * rows * 128, bytes_accessed=6 * MIB, transcendentals=0),
        name="faces_part",
    )(fields, prim)


def lines_kernel(flat, prim, weights_ref, terms, low_ref, high_ref, total):
    rows = flat.shape[1]
    half = rows // 2

    def fill(step, carry):
        at = pl.ds(pl.multiple_of(step * 32, 32), 32)
        v = prim[1, at, :]
        for field in range(FIELDS):
            flux = (prim[4, at, :] if field == 4 else flat[field, at, :]) * v
            if field == 2:
                flux = flux + prim[3, at, :]
            high, low = two_terms(flux)
            terms[field, at, 0:128] = high
            terms[field, at, 128:256] = low
        return carry

    lax.fori_loop(0, rows // 32, fill, 0)
    weights = weights_ref[...]
    for field in range(FIELDS):
        product = jnp.dot(terms[field], weights, preferred_element_type=F32)
        if field == 0:
            total[...] = product
        else:
            total[...] = jnp.where(lane_mask(field), product, total[...])
    value = total[...] * WHOLE_SCALE
    lanes = lax.broadcasted_iota(jnp.int32, (1, 128), 1)
    second = lanes % 64 >= 4 * FIELDS
    value = jnp.where(second, value - value.astype(BF16).astype(F32), value)
    turned = pltpu.roll(value, 64, 1)
    low_ref[...] = jnp.where(lanes < 64, value[0:half, :], turned[half:rows, :]).astype(BF16)
    high_ref[...] = jnp.where(lanes < 64, turned[0:half, :], value[half:rows, :]).astype(BF16)


def lines_part(flat, prim):
    rows = flat.shape[1]
    return pl.pallas_call(
        lines_kernel,
        in_specs=in_vmem(3),
        out_specs=in_vmem(3),
        out_shape=[
            jax.ShapeDtypeStruct((FIELDS, rows, 256), BF16),
            jax.ShapeDtypeStruct((rows // 2, 128), BF16),
            jax.ShapeDtypeStruct((rows // 2, 128), BF16),
        ],
        scratch_shapes=[pltpu.VMEM((rows, 128), F32)],
        compiler_params=pltpu.CompilerParams(vmem_limit_bytes=12 * MIB),
        cost_estimate=pl.CostEstimate(flops=300 * rows * 128, bytes_accessed=8 * MIB, transcendentals=0),
        name="lines_part",
    )(flat, prim, jnp.asarray(face_matrix(), BF16))


def sources(species, stress):
    moles = [species[k] * (18.0 / MOLAR_MASS[k]) for k in range(9)]
    summed = moles[0]
    for k in range(1, 9):
        summed = summed + moles[k]
    inverse_heat = UNIVERSAL_R * summed / stress
    e02 = jnp.exp(-0.2 * inverse_heat)
    e03 = jnp.exp(-0.3 * inverse_heat)
    e04 = e02 * e02
    e08 = e04 * e04
    e16 = e08 * e08
    powers = {0.2: e02, 0.3: e03, 0.4: e04, 0.8: e08, 1.6: e16}
    powers[1.2] = e08 * e04
    powers[1.8] = e16 * e02
    powers[2.0] = e16 * e04
    rates = [
        (step[3] * powers[step[4]]) * (moles[step[0]] * moles[step[1]]) for step in ARRHENIUS_LIST
    ]
    table = make_table()
    result = []
    for field in range(FIELDS):
        value = None
        for column in range(8):
            factor = float(table[field, column])
            if factor != 0.0:
                term = (TIME_STEP * factor) * rates[column]
                value = term if value is None else value + term
        result.append(value)
    return result


def windowed(flux, first, planes):
    window = {z: flux(z) for z in range(first - 4, first + 4)}
    for z in range(first, first + planes):
        window[z + 4] = flux(z + 4)
        change = None
        for m, weight in enumerate(CENTRAL_WEIGHTS, 1):
            term = (-TIME_STEP * weight) * (window[z + m] - window[z - m])
            change = term if change is None else change + term
        yield z, change


def inner_kernel(flat, prim, register, terms, line_ref, planes_ref, out, along_y):
    rows = flat.shape[1]
    depth = rows // 16

    def react(step, carry):
        at = pl.ds(pl.multiple_of(step * 32, 32), 32)
        made = sources([flat[5 + k, at, :] for k in range(9)], prim[3, at, :])
        for field in range(FIELDS):
            kept = SECTION_DECAY * register[field, at, :]
            out[field, at, :] = kept if made[field] is None else kept + made[field]
        return carry

    lax.fori_loop(0, rows // 32, react, 0)

    def along_x(flux):
        high, low = two_terms(flux)
        return jnp.dot(planes_ref[...], jnp.concatenate([high, low], axis=0), preferred_element_type=F32)

    def spread(field, carried):
        along_y[...] = jnp.dot(terms[field], line_ref[...], preferred_element_type=F32)
        for first in range(0, depth, 8):
            at = slice(first * 16, first * 16 + 128)
            both = along_y[at, :] + along_x(carried(at) * prim[0, at, :])
            out[field, at, :] += (-TIME_STEP * WHOLE_SCALE) * both
        for first in range(0, depth, 16):
            for row in (0, 8):

                def flux_z(z):
                    at = (z % depth) * 16 + row
                    return carried(slice(at, at + 8)) * prim[2, at : at + 8, :]

                for z, change in windowed(flux_z, first, 16):
                    at = slice(z * 16 + row, z * 16 + row + 8)
                    out[field, at, :] += change

    def across(index, carry):
        field = index + (index >= 4).astype(jnp.int32)
        spread(field, lambda at: flat[field, at, :])
        return carry

    lax.fori_loop(0, FIELDS - 1, across, 0)
    spread(4, lambda at: prim[4, at, :])

    for first in range(0, depth, 8):
        at = slice(first * 16, first * 16 + 128)
        out[1, at, :] += (-TIME_STEP * WHOLE_SCALE) * along_x(prim[3, at, :])
    for first in range(0, depth, 16):
        for row in (0, 8):

            def stress(z):
                at = (z % depth) * 16 + row
                return prim[3, at : at + 8, :]

            for z, change in windowed(stress, first, 16):
                at = slice(z * 16 + row, z * 16 + row + 8)
                out[3, at, :] += change


def inner_part(flat, prim, register, terms):
    rows = flat.shape[1]
    return pl.pallas_call(
        inner_kernel,
        in_specs=in_vmem(6),
        out_specs=pl.BlockSpec(memory_space=pltpu.VMEM),
        out_shape=jax.ShapeDtypeStruct((FIELDS, rows, 128), F32),
        scratch_shapes=[
            pltpu.VMEM((rows, 128), F32),
        ],
        compiler_params=pltpu.CompilerParams(vmem_limit_bytes=12 * MIB),
        cost_estimate=pl.CostEstimate(
            flops=2000 * rows * 128, bytes_accessed=20 * MIB, transcendentals=10 * rows * 128
        ),
        name="inner_part",
    )(flat, prim, register, terms, jnp.asarray(line_matrix(), BF16), jnp.asarray(planes_matrix(), BF16))


def outer_kernel(
    part, flat, prev, following, yprev, ynext, place_ref, fields_out, register_out,
    faces_x, along_y, message, fields_stage, register_stage, sent,
):
    rows = part.shape[1]
    depth = rows // 16
    half = rows // 2
    lanes = lax.broadcasted_iota(jnp.int32, (1, 128), 1)
    low = ynext[...].astype(F32)
    high = yprev[...].astype(F32)
    message[0:half, :] = jnp.where(lanes < 64, low, pltpu.roll(high, 64, 1)).astype(BF16)
    message[half:rows, :] = jnp.where(lanes < 64, pltpu.roll(low, 64, 1), high).astype(BF16)
    faces_x[...] = jnp.zeros(faces_x.shape, F32)
    place = place_ref[...]
    copies = []
    for field in range(FIELDS):
        for ref, layers in ((prev, (0, 1, 2, 3)), (following, (15, 14, 13, 12))):
            for cell, x in enumerate(layers):
                value = ref[4 * field + cell, :, :].astype(F32)
                if cell == 0 and field < FLOWS:
                    value = value + ref[4 * FIELDS + field, :, :].astype(F32)
                faces_x[pl.ds(x, depth, stride=16), :] = value
        held = message[...]
        picked = jnp.where(lane_mask(field), held, jnp.zeros_like(held))
        along_y[...] = jnp.dot(picked, place, preferred_element_type=F32)
        stored = part[field] - TIME_STEP * (along_y[...] + faces_x[...])
        register_stage[field] = stored
        fields_stage[field] = flat[field] + SECTION_WEIGHT * stored
        for index, (stage, ref) in enumerate(((register_stage, register_out), (fields_stage, fields_out))):
            copy = pltpu.make_async_copy(stage.at[field], ref.at[field], sent.at[index, field])
            copy.start()
            copies.append(copy)
    for copy in copies:
        copy.wait()


def outer_part(part, flat, prev, following, yprev, ynext):
    rows = flat.shape[1]
    return pl.pallas_call(
        outer_kernel,
        in_specs=in_vmem(7),
        out_specs=in_hbm(2),
        out_shape=[jax.ShapeDtypeStruct((FIELDS, rows, 128), F32)] * 2,
        scratch_shapes=[
            pltpu.VMEM((rows, 128), F32),
            pltpu.VMEM((rows, 128), F32),
            pltpu.VMEM((rows, 128), BF16),
            pltpu.VMEM((FIELDS, rows, 128), F32),
            pltpu.VMEM((FIELDS, rows, 128), F32),
            pltpu.SemaphoreType.DMA((2, FIELDS)),
        ],
        compiler_params=pltpu.CompilerParams(vmem_limit_bytes=20 * MIB),
        cost_estimate=pl.CostEstimate(
            flops=100 * rows * 128, bytes_accessed=24 * MIB, transcendentals=0
        ),
        name="outer_part",
    )(part, flat, prev, following, yprev, ynext, jnp.asarray(place_matrix(), BF16))


def lane_difference(values):
    lanes = lax.broadcasted_iota(jnp.int32, values[0].shape, 1)
    ahead = [pltpu.roll(value, 127, 1) for value in values]
    behind = [pltpu.roll(value, 1, 1) for value in values]
    count = len(values)
    return [
        jnp.where(lanes == 127, ahead[(j + 1) % count], ahead[j])
        - jnp.where(lanes == 0, behind[(j - 1) % count], behind[j])
        for j in range(count)
    ]


def inverse_length(a, b, c):
    return 1.0 * lax.rsqrt(jnp.maximum(a * a + b * b + c * c, GRAD_FLOOR * GRAD_FLOOR))


def unpack_kernel(count, own, blocks, scalar, speed, low_ref, high_ref, edge):
    edge[...] = jnp.zeros(edge.shape, F32)

    def body(j, carry):
        for z in range(own + 4):
            scalar[j, z * 32 + 8 : z * 32 + 24, :] = blocks[j, z * 16 : z * 16 + 16, :].astype(F32)
        for c in range(3):
            base = (own + 4 + c * (own + 2)) * 16
            for z in range(own + 2):
                speed[c, j, z * 32 + 8 : z * 32 + 24, :] = blocks[
                    j, base + z * 16 : base + z * 16 + 16, :
                ].astype(F32)
        for ref, first, second in ((low_ref, 8, 9), (high_ref, 23, 22)):
            edge[0 : own + 2, :] = scalar[j, pl.ds(32 + first, own + 2, stride=32), :]
            edge[own + 2 : 2 * own + 2, :] = scalar[j, pl.ds(64 + second, own, stride=32), :]
            for c in range(3):
                start = (c + 2) * own + 2
                edge[start : start + own, :] = speed[c, j, pl.ds(32 + first, own, stride=32), :]
            ref[j, :, :] = edge[...].astype(BF16)
        return carry

    lax.fori_loop(0, count, body, 0)


def unpack_part(blocks, own):
    count = blocks.shape[0]
    edge_rows = -(-(5 * own + 2) // 16) * 16
    return pl.pallas_call(
        functools.partial(unpack_kernel, count, own),
        in_specs=in_vmem(1),
        out_specs=in_vmem(4),
        out_shape=[
            jax.ShapeDtypeStruct((count, (own + 4) * 32, 128), F32),
            jax.ShapeDtypeStruct((3, count, (own + 2) * 32, 128), F32),
            jax.ShapeDtypeStruct((count, edge_rows, 128), BF16),
            jax.ShapeDtypeStruct((count, edge_rows, 128), BF16),
        ],
        scratch_shapes=[pltpu.VMEM((edge_rows, 128), F32)],
        compiler_params=pltpu.CompilerParams(vmem_limit_bytes=4 * MIB),
        cost_estimate=pl.CostEstimate(
            flops=10 * own * 16 * 128 * count, bytes_accessed=5 * MIB, transcendentals=0
        ),
        name="unpack_part",
    )(blocks)


def metrics_kernel(
    count, own, scalar_in, speed_in, prev, following, scalar, speed, out_ref, normal, normal_z, edge, stage, sent
):
    half = prev.shape[1]
    edge[:, 0:half, :] = prev[...].astype(F32)
    edge[:, half:, :] = following[...].astype(F32)
    for j in range(count):
        for side, row in ((0, 7), (half, 24)):
            scalar[j, pl.ds(32 + row, own + 2, stride=32), :] = edge[j, side : side + own + 2, :]
            for c in range(3):
                start = side + (c + 2) * own + 2
                speed[c, j, pl.ds(32 + row, own, stride=32), :] = edge[j, start : start + own, :]

    for side, inside, row in ((0, 8, 7), (half, 23, 24)):
        sign = 0.5 if row == 7 else -0.5
        lines = [edge[j, side + 1 : side + 1 + own, :] for j in range(count)]
        along_y = lane_difference(lines)
        for j in range(count):
            beyond = edge[j, side + own + 2 : side + 2 * own + 2, :]
            grad_x = sign * (scalar[j, pl.ds(64 + inside, own, stride=32), :] - beyond)
            grad_y = 0.5 * along_y[j]
            grad_z = 0.5 * (edge[j, side + 2 : side + 2 + own, :] - edge[j, side : side + own, :])
            normal[0, j, pl.ds(32 + row, own, stride=32), :] = -grad_x * inverse_length(
                grad_x, grad_y, grad_z
            )

    def window(z, row):
        return pl.ds(pl.multiple_of(z * 32, 32) + row, 16)

    def find_normals(z, carry):
        along_y = lane_difference([scalar[j, window(z + 1, 8), :] for j in range(count)])
        for j in range(count):
            grad_x = 0.5 * (scalar[j, window(z + 1, 9), :] - scalar[j, window(z + 1, 7), :])
            grad_y = 0.5 * along_y[j]
            grad_z = 0.5 * (scalar[j, window(z + 2, 8), :] - scalar[j, window(z, 8), :])
            scale = -inverse_length(grad_x, grad_y, grad_z)
            normal[0, j, window(z, 8), :] = grad_x * scale
            normal[1, j, window(z, 8), :] = grad_y * scale
            normal_z[j, z, :, :] = grad_z * scale
        return carry

    lax.fori_loop(0, own + 2, find_normals, 0)

    def find_metrics(z, carry):
        curve_y = lane_difference([normal[1, j, window(z + 1, 8), :] for j in range(count)])
        speed_y = [
            lane_difference([speed[c, j, window(z + 1, 8), :] for j in range(count)])
            for c in range(3)
        ]
        for j in range(count):
            lanes = slice(j * 128, j * 128 + 128)
            normals = [
                normal[0, j, window(z + 1, 8), :],
                normal[1, j, window(z + 1, 8), :],
                normal_z[j, z + 1, :, :],
            ]
            curvature = 0.5 * (
                (normal[0, j, window(z + 1, 9), :] - normal[0, j, window(z + 1, 7), :])
                + curve_y[j]
                + (normal_z[j, z + 2, :, :] - normal_z[j, z, :, :])
            )
            strain = None
            for c in range(3):
                slopes = [
                    speed[c, j, window(z + 1, 9), :] - speed[c, j, window(z + 1, 7), :],
                    speed_y[c][j],
                    speed[c, j, window(z + 2, 8), :] - speed[c, j, window(z, 8), :],
                ]
                along = normals[0] * slopes[0] + normals[1] * slopes[1] + normals[2] * slopes[2]
                term = slopes[c] - normals[c] * along
                strain = term if strain is None else strain + term
            for index, value in enumerate(normals + [curvature, 0.5 * strain]):
                stage[index, z, :, lanes] = value.astype(BF16)
        pltpu.make_async_copy(stage.at[:, z], out_ref.at[:, z], sent.at[z]).start()
        return carry

    lax.fori_loop(0, own, find_metrics, 0)
    for z in range(own):
        pltpu.make_async_copy(stage.at[:, z], out_ref.at[:, z], sent.at[z]).wait()


def metrics_part(scalar, speed, prev, following, own):
    count, half = prev.shape[:2]
    shape = (5, own, 16, count * 128)
    return pl.pallas_call(
        functools.partial(metrics_kernel, count, own),
        in_specs=in_vmem(4),
        out_specs=in_vmem(2) + in_hbm(1),
        out_shape=[
            jax.ShapeDtypeStruct(scalar.shape, F32),
            jax.ShapeDtypeStruct(speed.shape, F32),
            jax.ShapeDtypeStruct(shape, BF16),
        ],
        input_output_aliases={0: 0, 1: 1},
        scratch_shapes=[
            pltpu.VMEM((2, count, (own + 2) * 32, 128), F32),
            pltpu.VMEM((count, own + 2, 16, 128), F32),
            pltpu.VMEM((count, 2 * half, 128), F32),
            pltpu.VMEM(shape, BF16),
            pltpu.SemaphoreType.DMA((own,)),
        ],
        compiler_params=pltpu.CompilerParams(vmem_limit_bytes=10 * MIB),
        cost_estimate=pl.CostEstimate(
            flops=300 * own * 16 * 128 * count, bytes_accessed=3 * MIB, transcendentals=0
        ),
        name="flame_metrics",
    )(scalar, speed, prev, following)[2]


def per_device(fields, register):
    depth, count_x, count_y = fields.shape[1:]
    given = fields.reshape(FIELDS, depth * count_x, count_y)
    count = lax.axis_size("gy")
    own = depth // count
    x_forward, x_backward = ring("gx")
    y_forward, y_backward = ring("gy")

    prim, main = probe_part(given, count)
    blocks = lax.all_to_all(main, "gy", 0, 0, tiled=True)
    flat, low, high = faces_part(given, prim)
    following = lax.ppermute(low, "gx", x_backward)
    prev = lax.ppermute(high, "gx", x_forward)
    terms, ylow, yhigh = lines_part(flat, prim)
    ynext = lax.ppermute(ylow, "gy", y_backward)
    yprev = lax.ppermute(yhigh, "gy", y_forward)
    part = inner_part(flat, prim, register.reshape(flat.shape), terms)
    blocks, part = lax.optimization_barrier((blocks, part))
    scalar, speed, edge_low, edge_high = unpack_part(blocks, own)
    edge_prev = lax.ppermute(edge_high, "gx", x_forward)
    edge_next = lax.ppermute(edge_low, "gx", x_backward)
    part, scalar = lax.optimization_barrier((part, scalar))
    fields_next, register_next = outer_part(part, flat, prev, following, yprev, ynext)
    metrics = metrics_part(scalar, speed, edge_prev, edge_next, own)
    return (fields_next.reshape(fields.shape), register_next.reshape(fields.shape), metrics)


def solution(mesh):
    in_specs = (P(None, None, "gx", "gy"), P(None, None, "gx", "gy"))
    out_specs = (P(None, None, "gx", "gy"), P(None, None, "gx", "gy"), P(None, "gy", "gx", None))
    return jax.shard_map(
        per_device, mesh=mesh, in_specs=in_specs, out_specs=out_specs, check_vma=False
    )
```

```python
import functools

import jax
import jax.numpy as jnp
import numpy as np
from jax import lax
from jax.experimental import pallas as pl
from jax.experimental.pallas import tpu as pltpu
from jax.sharding import PartitionSpec as P

GAMMA_LESS = 0.4
UNIVERSAL_R = 0.25
TIME_STEP = 0.25
SECTION_DECAY = -0.4178904745
SECTION_WEIGHT = 0.3792103129
GRAD_FLOOR = 0.1
PROGRESS_SCALE = 4.0
CENTRAL_WEIGHTS = (0.8, -0.2, 4.0 / 105.0, -1.0 / 280.0)
WHOLE_WEIGHTS = (672.0, -168.0, 32.0, -3.0)
WHOLE_SCALE = 1.0 / 840.0
MOLAR_MASS = (2.0, 32.0, 16.0, 17.0, 18.0, 1.0, 33.0, 34.0, 28.0)
FORMATION_HEAT = (0.0, 0.0, 2.0, 0.3, -1.5, 3.0, 0.1, -0.4, 0.0)
ARRHENIUS_LIST = (
    (5, 1, (2, 3), 40.0, 2.0),
    (2, 0, (5, 3), 30.0, 1.2),
    (3, 0, (5, 4), 25.0, 0.8),
    (2, 4, (3, 3), 10.0, 1.6),
    (5, 1, (6,), 15.0, 0.2),
    (6, 5, (3, 3), 20.0, 0.3),
    (6, 6, (7, 1), 12.0, 0.4),
    (7, 8, (3, 3, 8), 8.0, 1.8),
)
FIELDS = 14
FLOWS = 5
LAYERS = 4 * FIELDS + FLOWS
FIRST = 5
MIB = 1 << 20
LONG = pl.CostEstimate(flops=10**10, bytes_accessed=10**6, transcendentals=0)
F32 = jnp.float32
BF16 = jnp.bfloat16


def make_table():
    table = np.zeros((14, 8))
    for column, step in enumerate(ARRHENIUS_LIST):
        change = np.zeros(9)
        change[step[0]] -= 1.0
        change[step[1]] -= 1.0
        for product in step[2]:
            change[product] += 1.0
        for species in range(9):
            mass_change = MOLAR_MASS[species] / 18.0 * change[species]
            table[5 + species, column] = mass_change
            table[4, column] -= FORMATION_HEAT[species] * mass_change
    return table


def ring(axis, distance):
    count = lax.axis_size(axis)
    return [(i, (i + distance) % count) for i in range(count)]


def lane_cell(lane):
    place = lane % 64
    return place % 4 if place < 4 * FIELDS else 0


def face_matrix():
    weights = np.zeros((128, 128), np.float32)
    for lane in range(64):
        cell = lane_cell(lane)
        for k in range(4 - cell):
            weights[k, lane] = WHOLE_WEIGHTS[k + cell]
            weights[127 - k, 64 + lane] = -WHOLE_WEIGHTS[k + cell]
    return np.concatenate([weights, weights], axis=0)


def place_matrix():
    weights = np.zeros((128, 128), np.float32)
    for lane in range(64):
        cell = lane_cell(lane)
        weights[lane, 127 - cell] = 1.0
        weights[64 + lane, cell] = 1.0
    return weights


def line_matrix():
    weights = np.zeros((128, 128), np.float32)
    for out in range(128):
        for m in range(1, 5):
            if out + m < 128:
                weights[out + m, out] = WHOLE_WEIGHTS[m - 1]
            if out - m >= 0:
                weights[out - m, out] = -WHOLE_WEIGHTS[m - 1]
    return np.concatenate([weights, weights], axis=0)


def planes_matrix():
    weights = np.zeros((128, 128), np.float32)
    for out in range(128):
        for m in range(1, 5):
            if out % 16 + m < 16:
                weights[out, out + m] = WHOLE_WEIGHTS[m - 1]
            if out % 16 - m >= 0:
                weights[out, out - m] = -WHOLE_WEIGHTS[m - 1]
    return np.concatenate([weights, weights], axis=1)


def lane_mask(field):
    lanes = lax.broadcasted_iota(jnp.int32, (1, 128), 1) % 64
    mask = (lanes >= 4 * field) & (lanes < 4 * field + 4)
    if field < FLOWS:
        mask = mask | (lanes == 4 * FIELDS + field)
    return mask


def two_terms(value):
    high = value.astype(BF16)
    low = (value - high.astype(F32)).astype(BF16)
    return high, low


def in_vmem(count):
    return [pl.BlockSpec(memory_space=pltpu.VMEM)] * count


def in_hbm(count):
    return [pl.BlockSpec(memory_space=pltpu.HBM)] * count


def probe_kernel(count, fields_ref, prim, *refs):
    blocks, (held, progress, arrived) = refs[:count], refs[count:]
    rows = prim.shape[1]
    depth = rows // 16
    own = depth // count
    chunk = 256

    def arrival(step):
        there = pl.ds(pl.multiple_of(step * chunk, chunk), chunk)
        return [
            pltpu.make_async_copy(
                fields_ref.at[0:5, there, :], held.at[0:5, there, :], arrived.at[0, step]
            ),
            pltpu.make_async_copy(
                fields_ref.at[9, there, :], held.at[5, there, :], arrived.at[1, step]
            ),
        ]

    for step in range(rows // chunk):
        for copy in arrival(step):
            copy.start()

    def chunk_body(step, carry):
        for copy in arrival(step):
            copy.wait()

        def fill(part, inner_carry):
            at = pl.ds(pl.multiple_of(step * chunk + part * 64, 64), 64)
            density = held[0, at, :]
            mx, my, mz, energy = [held[c, at, :] for c in range(1, 5)]
            u, v, w = mx / density, my / density, mz / density
            stress = GAMMA_LESS * (energy - 0.5 * (mx * u + my * v + mz * w))
            progress[at, :] = PROGRESS_SCALE * (held[5, at, :] / density)
            prim[0, at, :] = u
            prim[1, at, :] = v
            prim[2, at, :] = w
            prim[3, at, :] = stress
            prim[4, at, :] = energy + stress
            return inner_carry

        lax.fori_loop(0, chunk // 64, fill, 0)
        return carry

    lax.fori_loop(0, rows // chunk, chunk_body, 0)

    me = lax.axis_index("gy")
    for distance in range(count):
        first = own * lax.rem(me + distance, count) + depth
        offset = 0
        for c in range(4):
            margin = 2 if c == 0 else 1
            for z in range(-margin, own + margin):
                at = pl.ds(pl.multiple_of(lax.rem(first + z, depth) * 16, 16), 16)
                plane = progress[at, :] if c == 0 else prim[c - 1, at, :]
                blocks[distance][offset : offset + 16, :] = plane.astype(BF16)
                offset += 16


def probe_part(fields, count):
    rows = fields.shape[1]
    own = rows // 16 // count
    main_rows = (4 * own + 10) * 16
    return pl.pallas_call(
        functools.partial(probe_kernel, count),
        in_specs=in_hbm(1),
        out_specs=in_vmem(1 + count),
        out_shape=[jax.ShapeDtypeStruct((5, rows, 128), F32)]
        + [jax.ShapeDtypeStruct((main_rows, 128), BF16)] * count,
        scratch_shapes=[
            pltpu.VMEM((6, rows, 128), F32),
            pltpu.VMEM((rows, 128), F32),
            pltpu.SemaphoreType.DMA((2, rows // 256)),
        ],
        compiler_params=pltpu.CompilerParams(vmem_limit_bytes=48 * MIB),
        cost_estimate=LONG,
        name="probe_part",
    )(fields)


def faces_kernel(fields_ref, prim, flat, low_ref, high_ref, arrived):
    rows = flat.shape[1]

    def arrival(step):
        there = pl.ds(pl.multiple_of(step * 256, 256), 256)
        return pltpu.make_async_copy(
            fields_ref.at[:, there, :], flat.at[:, there, :], arrived.at[step]
        )

    for step in range(rows // 256):
        arrival(step).start()

    def chunk_body(step, carry):
        arrival(step).wait()
        planes = pl.ds(pl.multiple_of(step * 16, 16), 16)

        def layer(ref, index, x):
            return ref[index, pl.ds(step * 256 + x, 16, stride=16), :]

        for ref, layers, sign in ((low_ref, (0, 1, 2, 3), 1.0), (high_ref, (15, 14, 13, 12), -1.0)):
            speeds = [layer(prim, 0, x) for x in layers]
            for field in range(FIELDS):
                source = (prim, 4) if field == 4 else (flat, field)
                flux = [layer(*source, x) * speeds[k] for k, x in enumerate(layers)]
                if field == 1:
                    flux = [flux[k] + layer(prim, 3, x) for k, x in enumerate(layers)]
                for cell in range(4):
                    part = (sign * CENTRAL_WEIGHTS[cell]) * flux[0]
                    for k in range(1, 4 - cell):
                        part = part + (sign * CENTRAL_WEIGHTS[k + cell]) * flux[k]
                    high, low = two_terms(part)
                    ref[4 * field + cell, planes, :] = high
                    if cell == 0 and field < FLOWS:
                        ref[4 * FIELDS + field, planes, :] = low
        return carry

    lax.fori_loop(0, rows // 256, chunk_body, 0)


def faces_part(fields, prim):
    rows = fields.shape[1]
    depth = rows // 16
    return pl.pallas_call(
        faces_kernel,
        in_specs=in_hbm(1) + in_vmem(1),
        out_specs=in_vmem(3),
        out_shape=[
            jax.ShapeDtypeStruct(fields.shape, F32),
            jax.ShapeDtypeStruct((LAYERS, depth, 128), BF16),
            jax.ShapeDtypeStruct((LAYERS, depth, 128), BF16),
        ],
        scratch_shapes=[pltpu.SemaphoreType.DMA((rows // 256,))],
        compiler_params=pltpu.CompilerParams(vmem_limit_bytes=40 * MIB),
        cost_estimate=LONG,
        name="faces_part",
    )(fields, prim)


def lines_kernel(flat, prim, weights_ref, low_block, high_block, terms, low_ref, high_ref, total):
    start = low_block.shape[0]
    low_ref[0:start, :] = low_block[...]
    high_ref[0:start, :] = high_block[...]
    rows = flat.shape[1]
    half = rows // 2

    def fill(step, carry):
        at = pl.ds(pl.multiple_of(step * 32, 32), 32)
        v = prim[1, at, :]
        for field in range(FIELDS):
            flux = (prim[4, at, :] if field == 4 else flat[field, at, :]) * v
            if field == 2:
                flux = flux + prim[3, at, :]
            high, low = two_terms(flux)
            terms[field, at, 0:128] = high
            terms[field, at, 128:256] = low
        return carry

    lax.fori_loop(0, rows // 32, fill, 0)
    weights = weights_ref[...]
    for field in range(FIELDS):
        product = jnp.dot(terms[field], weights, preferred_element_type=F32)
        if field == 0:
            total[...] = product
        else:
            total[...] = jnp.where(lane_mask(field), product, total[...])
    value = total[...] * WHOLE_SCALE
    lanes = lax.broadcasted_iota(jnp.int32, (1, 128), 1)
    second = lanes % 64 >= 4 * FIELDS
    value = jnp.where(second, value - value.astype(BF16).astype(F32), value)
    turned = pltpu.roll(value, 64, 1)
    low_ref[start:, :] = jnp.where(lanes < 64, value[0:half, :], turned[half:rows, :]).astype(BF16)
    high_ref[start:, :] = jnp.where(lanes < 64, turned[0:half, :], value[half:rows, :]).astype(BF16)


def lines_part(flat, prim, low_block, high_block):
    rows = flat.shape[1]
    message = low_block.shape[0] + rows // 2
    return pl.pallas_call(
        lines_kernel,
        in_specs=in_vmem(5),
        out_specs=in_vmem(3),
        out_shape=[
            jax.ShapeDtypeStruct((FIELDS, rows, 256), BF16),
            jax.ShapeDtypeStruct((message, 128), BF16),
            jax.ShapeDtypeStruct((message, 128), BF16),
        ],
        scratch_shapes=[pltpu.VMEM((rows, 128), F32)],
        compiler_params=pltpu.CompilerParams(vmem_limit_bytes=12 * MIB),
        cost_estimate=LONG,
        name="lines_part",
    )(flat, prim, jnp.asarray(face_matrix(), BF16), low_block, high_block)


def sources(species, stress):
    moles = [species[k] * (18.0 / MOLAR_MASS[k]) for k in range(9)]
    summed = moles[0]
    for k in range(1, 9):
        summed = summed + moles[k]
    inverse_heat = UNIVERSAL_R * summed / stress
    e02 = jnp.exp(-0.2 * inverse_heat)
    e03 = jnp.exp(-0.3 * inverse_heat)
    e04 = e02 * e02
    e08 = e04 * e04
    e16 = e08 * e08
    powers = {0.2: e02, 0.3: e03, 0.4: e04, 0.8: e08, 1.6: e16}
    powers[1.2] = e08 * e04
    powers[1.8] = e16 * e02
    powers[2.0] = e16 * e04
    rates = [
        (step[3] * powers[step[4]]) * (moles[step[0]] * moles[step[1]]) for step in ARRHENIUS_LIST
    ]
    table = make_table()
    result = []
    for field in range(FIELDS):
        value = None
        for column in range(8):
            factor = float(table[field, column])
            if factor != 0.0:
                term = (TIME_STEP * factor) * rates[column]
                value = term if value is None else value + term
        result.append(value)
    return result


def windowed(flux, first, planes):
    window = {z: flux(z) for z in range(first - 4, first + 4)}
    for z in range(first, first + planes):
        window[z + 4] = flux(z + 4)
        change = None
        for m, weight in enumerate(CENTRAL_WEIGHTS, 1):
            term = (-TIME_STEP * weight) * (window[z + m] - window[z - m])
            change = term if change is None else change + term
        yield z, change


def inner_kernel(flat, prim, register, terms, line_ref, planes_ref, out, along_y):
    rows = flat.shape[1]
    depth = rows // 16

    def react(step, carry):
        at = pl.ds(pl.multiple_of(step * 32, 32), 32)
        made = sources([flat[5 + k, at, :] for k in range(9)], prim[3, at, :])
        for field in range(FIELDS):
            kept = SECTION_DECAY * register[field, at, :]
            out[field, at, :] = kept if made[field] is None else kept + made[field]
        return carry

    lax.fori_loop(0, rows // 32, react, 0)

    def along_x(flux):
        high, low = two_terms(flux)
        return jnp.dot(planes_ref[...], jnp.concatenate([high, low], axis=0), preferred_element_type=F32)

    def spread(field, carried):
        along_y[...] = jnp.dot(terms[field], line_ref[...], preferred_element_type=F32)
        for first in range(0, depth, 8):
            at = slice(first * 16, first * 16 + 128)
            both = along_y[at, :] + along_x(carried(at) * prim[0, at, :])
            out[field, at, :] += (-TIME_STEP * WHOLE_SCALE) * both
        for first in range(0, depth, 16):
            for row in (0, 8):

                def flux_z(z):
                    at = (z % depth) * 16 + row
                    return carried(slice(at, at + 8)) * prim[2, at : at + 8, :]

                for z, change in windowed(flux_z, first, 16):
                    at = slice(z * 16 + row, z * 16 + row + 8)
                    out[field, at, :] += change

    def across(index, carry):
        field = index + (index >= 4).astype(jnp.int32)
        spread(field, lambda at: flat[field, at, :])
        return carry

    lax.fori_loop(0, FIELDS - 1, across, 0)
    spread(4, lambda at: prim[4, at, :])

    for first in range(0, depth, 8):
        at = slice(first * 16, first * 16 + 128)
        out[1, at, :] += (-TIME_STEP * WHOLE_SCALE) * along_x(prim[3, at, :])
    for first in range(0, depth, 16):
        for row in (0, 8):

            def stress(z):
                at = (z % depth) * 16 + row
                return prim[3, at : at + 8, :]

            for z, change in windowed(stress, first, 16):
                at = slice(z * 16 + row, z * 16 + row + 8)
                out[3, at, :] += change


def inner_part(flat, prim, register, terms):
    rows = flat.shape[1]
    return pl.pallas_call(
        inner_kernel,
        in_specs=in_vmem(6),
        out_specs=pl.BlockSpec(memory_space=pltpu.VMEM),
        out_shape=jax.ShapeDtypeStruct((FIELDS, rows, 128), F32),
        scratch_shapes=[
            pltpu.VMEM((rows, 128), F32),
        ],
        compiler_params=pltpu.CompilerParams(vmem_limit_bytes=12 * MIB),
        cost_estimate=LONG,
        name="inner_part",
    )(flat, prim, register, terms, jnp.asarray(line_matrix(), BF16), jnp.asarray(planes_matrix(), BF16))


def add_faces(
    chosen, part, flat, prev, following, yprev, ynext, place_ref, fields_out, register_out,
    faces_x, along_y, message, fields_stage, register_stage, sent,
):
    rows = part.shape[1]
    depth = rows // 16
    half = rows // 2
    lanes = lax.broadcasted_iota(jnp.int32, (1, 128), 1)
    start = ynext.shape[0] - half
    low = ynext[start:, :].astype(F32)
    high = yprev[start:, :].astype(F32)
    message[0:half, :] = jnp.where(lanes < 64, low, pltpu.roll(high, 64, 1)).astype(BF16)
    message[half:rows, :] = jnp.where(lanes < 64, pltpu.roll(low, 64, 1), high).astype(BF16)
    faces_x[...] = jnp.zeros(faces_x.shape, F32)
    place = place_ref[...]
    copies = []
    for slot, field in enumerate(chosen):
        for ref, layers in ((prev, (0, 1, 2, 3)), (following, (15, 14, 13, 12))):
            for cell, x in enumerate(layers):
                value = ref[4 * field + cell, :, :].astype(F32)
                if cell == 0 and field < FLOWS:
                    value = value + ref[4 * FIELDS + field, :, :].astype(F32)
                faces_x[pl.ds(x, depth, stride=16), :] = value
        held = message[...]
        picked = jnp.where(lane_mask(field), held, jnp.zeros_like(held))
        along_y[...] = jnp.dot(picked, place, preferred_element_type=F32)
        stored = part[field] - TIME_STEP * (along_y[...] + faces_x[...])
        register_stage[slot] = stored
        fields_stage[slot] = flat[field] + SECTION_WEIGHT * stored
        for index, (stage, ref) in enumerate(((register_stage, register_out), (fields_stage, fields_out))):
            copy = pltpu.make_async_copy(stage.at[slot], ref.at[field], sent.at[index, slot])
            copy.start()
            copies.append(copy)
    return copies


def faces_scratch(number, rows):
    return [
        pltpu.VMEM((rows, 128), F32),
        pltpu.VMEM((rows, 128), F32),
        pltpu.VMEM((rows, 128), BF16),
        pltpu.VMEM((number, rows, 128), F32),
        pltpu.VMEM((number, rows, 128), F32),
        pltpu.SemaphoreType.DMA((2, number)),
    ]


def outer_kernel(chosen, *refs):
    for copy in add_faces(chosen, *refs):
        copy.wait()


def outer_part(chosen, operands):
    rows = operands[0].shape[1]
    return pl.pallas_call(
        functools.partial(outer_kernel, chosen),
        in_specs=in_vmem(7),
        out_specs=in_hbm(2),
        out_shape=[jax.ShapeDtypeStruct((FIELDS, rows, 128), F32)] * 2,
        scratch_shapes=faces_scratch(len(chosen), rows),
        compiler_params=pltpu.CompilerParams(vmem_limit_bytes=12 * MIB),
        cost_estimate=LONG,
        name="outer_part",
    )(*operands)


def lane_difference(values):
    lanes = lax.broadcasted_iota(jnp.int32, values[0].shape, 1)
    ahead = [pltpu.roll(value, 127, 1) for value in values]
    behind = [pltpu.roll(value, 1, 1) for value in values]
    count = len(values)
    return [
        jnp.where(lanes == 127, ahead[(j + 1) % count], ahead[j])
        - jnp.where(lanes == 0, behind[(j - 1) % count], behind[j])
        for j in range(count)
    ]


def in_pairs(total, work):
    together = 2 if total % 2 == 0 else 1

    def body(step, carry):
        for offset in range(together):
            work(step * together + offset)
        return carry

    lax.fori_loop(0, total // together, body, 0)


def inverse_length(a, b, c):
    return 1.0 * lax.rsqrt(jnp.maximum(a * a + b * b + c * c, GRAD_FLOOR * GRAD_FLOOR))


def unpack_kernel(count, own, *refs):
    blocks, (scalar, speed, low_ref, high_ref, edge) = refs[:count], refs[count:]
    edge[...] = jnp.zeros(edge.shape, F32)
    me = lax.axis_index("gy")
    for distance, block in enumerate(blocks):
        j = lax.rem(me - distance + count, count)
        for z in range(own + 4):
            scalar[j, z * 32 + 8 : z * 32 + 24, :] = block[z * 16 : z * 16 + 16, :].astype(F32)
        for c in range(3):
            base = (own + 4 + c * (own + 2)) * 16
            for z in range(own + 2):
                speed[c, j, z * 32 + 8 : z * 32 + 24, :] = block[
                    base + z * 16 : base + z * 16 + 16, :
                ].astype(F32)
        for ref, first, second in ((low_ref, 8, 9), (high_ref, 23, 22)):
            edge[0 : own + 2, :] = scalar[j, pl.ds(32 + first, own + 2, stride=32), :]
            edge[own + 2 : 2 * own + 2, :] = scalar[j, pl.ds(64 + second, own, stride=32), :]
            for c in range(3):
                start = (c + 2) * own + 2
                edge[start : start + own, :] = speed[c, j, pl.ds(32 + first, own, stride=32), :]
            ref[j, :, :] = edge[...].astype(BF16)


def unpack_part(blocks, own):
    count = len(blocks)
    edge_rows = -(-(5 * own + 2) // 16) * 16
    return pl.pallas_call(
        functools.partial(unpack_kernel, count, own),
        in_specs=in_vmem(count),
        out_specs=in_vmem(4),
        out_shape=[
            jax.ShapeDtypeStruct((count, (own + 4) * 32, 128), F32),
            jax.ShapeDtypeStruct((3, count, (own + 2) * 32, 128), F32),
            jax.ShapeDtypeStruct((count, edge_rows, 128), BF16),
            jax.ShapeDtypeStruct((count, edge_rows, 128), BF16),
        ],
        scratch_shapes=[pltpu.VMEM((edge_rows, 128), F32)],
        compiler_params=pltpu.CompilerParams(vmem_limit_bytes=4 * MIB),
        cost_estimate=LONG,
        name="unpack_part",
    )(*blocks)


def finish_kernel(count, own, chosen, *refs):
    operands, refs = refs[:7], refs[7:]
    scalar_in, speed_in, prev, following, _, _ = refs[:6]
    fields_out, register_out, scalar, speed, out_ref = refs[6:11]
    scratch, (normal, normal_z, edge, stage, sent) = refs[11:17], refs[17:]
    copies = add_faces(chosen, *operands, fields_out, register_out, *scratch)
    half = prev.shape[1]
    edge[:, 0:half, :] = prev[...].astype(F32)
    edge[:, half:, :] = following[...].astype(F32)
    for j in range(count):
        for side, row in ((0, 7), (half, 24)):
            scalar[j, pl.ds(32 + row, own + 2, stride=32), :] = edge[j, side : side + own + 2, :]
            for c in range(3):
                start = side + (c + 2) * own + 2
                speed[c, j, pl.ds(32 + row, own, stride=32), :] = edge[j, start : start + own, :]

    for side, inside, row in ((0, 8, 7), (half, 23, 24)):
        sign = 0.5 if row == 7 else -0.5
        lines = [edge[j, side + 1 : side + 1 + own, :] for j in range(count)]
        along_y = lane_difference(lines)
        for j in range(count):
            beyond = edge[j, side + own + 2 : side + 2 * own + 2, :]
            grad_x = sign * (scalar[j, pl.ds(64 + inside, own, stride=32), :] - beyond)
            grad_y = 0.5 * along_y[j]
            grad_z = 0.5 * (edge[j, side + 2 : side + 2 + own, :] - edge[j, side : side + own, :])
            normal[0, j, pl.ds(32 + row, own, stride=32), :] = -grad_x * inverse_length(
                grad_x, grad_y, grad_z
            )

    def window(z, row):
        return pl.ds(pl.multiple_of(z * 32, 32) + row, 16)

    def find_normals(z):
        along_y = lane_difference([scalar[j, window(z + 1, 8), :] for j in range(count)])
        for j in range(count):
            grad_x = 0.5 * (scalar[j, window(z + 1, 9), :] - scalar[j, window(z + 1, 7), :])
            grad_y = 0.5 * along_y[j]
            grad_z = 0.5 * (scalar[j, window(z + 2, 8), :] - scalar[j, window(z, 8), :])
            scale = -inverse_length(grad_x, grad_y, grad_z)
            normal[0, j, window(z, 8), :] = grad_x * scale
            normal[1, j, window(z, 8), :] = grad_y * scale
            normal_z[j, z, :, :] = grad_z * scale

    in_pairs(own + 2, find_normals)

    def find_metrics(z):
        curve_y = lane_difference([normal[1, j, window(z + 1, 8), :] for j in range(count)])
        speed_y = [
            lane_difference([speed[c, j, window(z + 1, 8), :] for j in range(count)])
            for c in range(3)
        ]
        for j in range(count):
            lanes = slice(j * 128, j * 128 + 128)
            normals = [
                normal[0, j, window(z + 1, 8), :],
                normal[1, j, window(z + 1, 8), :],
                normal_z[j, z + 1, :, :],
            ]
            curvature = 0.5 * (
                (normal[0, j, window(z + 1, 9), :] - normal[0, j, window(z + 1, 7), :])
                + curve_y[j]
                + (normal_z[j, z + 2, :, :] - normal_z[j, z, :, :])
            )
            strain = None
            for c in range(3):
                slopes = [
                    speed[c, j, window(z + 1, 9), :] - speed[c, j, window(z + 1, 7), :],
                    speed_y[c][j],
                    speed[c, j, window(z + 2, 8), :] - speed[c, j, window(z, 8), :],
                ]
                along = normals[0] * slopes[0] + normals[1] * slopes[1] + normals[2] * slopes[2]
                term = slopes[c] - normals[c] * along
                strain = term if strain is None else strain + term
            for index, value in enumerate(normals + [curvature, 0.5 * strain]):
                stage[index, z, :, lanes] = value.astype(BF16)
        pltpu.make_async_copy(stage.at[:, z], out_ref.at[:, z], sent.at[z]).start()

    in_pairs(own, find_metrics)
    for copy in copies:
        copy.wait()
    for z in range(own):
        pltpu.make_async_copy(stage.at[:, z], out_ref.at[:, z], sent.at[z]).wait()


def finish_part(chosen, operands, scalar, speed, prev, following, fields, register, own):
    count, half = prev.shape[:2]
    rows = fields.shape[1]
    shape = (5, own, 16, count * 128)
    fields, register, _, _, metrics = pl.pallas_call(
        functools.partial(finish_kernel, count, own, chosen),
        in_specs=in_vmem(11) + in_hbm(2),
        out_specs=in_hbm(2) + in_vmem(2) + in_hbm(1),
        out_shape=[
            jax.ShapeDtypeStruct(fields.shape, F32),
            jax.ShapeDtypeStruct(register.shape, F32),
            jax.ShapeDtypeStruct(scalar.shape, F32),
            jax.ShapeDtypeStruct(speed.shape, F32),
            jax.ShapeDtypeStruct(shape, BF16),
        ],
        input_output_aliases={7: 2, 8: 3, 11: 0, 12: 1},
        scratch_shapes=faces_scratch(len(chosen), rows)
        + [
            pltpu.VMEM((2, count, (own + 2) * 32, 128), F32),
            pltpu.VMEM((count, own + 2, 16, 128), F32),
            pltpu.VMEM((count, 2 * half, 128), F32),
            pltpu.VMEM(shape, BF16),
            pltpu.SemaphoreType.DMA((own,)),
        ],
        compiler_params=pltpu.CompilerParams(vmem_limit_bytes=20 * MIB),
        cost_estimate=LONG,
        name="finish_part",
    )(*operands, scalar, speed, prev, following, fields, register)
    return fields, register, metrics


def per_device(fields, register):
    depth, count_x, count_y = fields.shape[1:]
    given = fields.reshape(FIELDS, depth * count_x, count_y)
    count = lax.axis_size("gy")
    own = depth // count
    x_forward, x_backward = ring("gx", 1), ring("gx", -1)

    prim, *blocks = probe_part(given, count)
    for distance in range(2, count - 1):
        blocks[distance] = lax.ppermute(blocks[distance], "gy", ring("gy", distance))
    flat, low, high = faces_part(given, prim)
    terms, to_prev, to_next = lines_part(flat, prim, blocks[count - 1], blocks[1])
    blocks[count - 1] = lax.ppermute(to_prev, "gy", ring("gy", -1))
    blocks[1] = lax.ppermute(to_next, "gy", ring("gy", 1))
    low, high, terms = lax.optimization_barrier((low, high, terms))
    following = lax.ppermute(low, "gx", x_backward)
    prev = lax.ppermute(high, "gx", x_forward)
    part = inner_part(flat, prim, register.reshape(flat.shape), terms)
    *blocks, part = lax.optimization_barrier((*blocks, part))
    scalar, speed, edge_low, edge_high = unpack_part(blocks, own)
    edge_prev = lax.ppermute(edge_high, "gx", x_forward)
    edge_next = lax.ppermute(edge_low, "gx", x_backward)
    part, scalar = lax.optimization_barrier((part, scalar))
    operands = (
        part, flat, prev, following, blocks[1], blocks[count - 1], jnp.asarray(place_matrix(), BF16)
    )
    first, last = tuple(range(FIRST)), tuple(range(FIRST, FIELDS))
    fields_next, register_next = outer_part(first, operands)
    edge_prev, edge_next, fields_next = lax.optimization_barrier((edge_prev, edge_next, fields_next))
    fields_next, register_next, metrics = finish_part(
        last, operands, scalar, speed, edge_prev, edge_next, fields_next, register_next, own
    )
    return (fields_next.reshape(fields.shape), register_next.reshape(fields.shape), metrics)


def solution(mesh):
    in_specs = (P(None, None, "gx", "gy"), P(None, None, "gx", "gy"))
    out_specs = (P(None, None, "gx", "gy"), P(None, None, "gx", "gy"), P(None, "gy", "gx", None))
    return jax.shard_map(
        per_device, mesh=mesh, in_specs=in_specs, out_specs=out_specs, check_vma=False
    )
```

```python
import functools

import jax
import jax.numpy as jnp
import numpy as np
from jax import lax
from jax.experimental import pallas as pl
from jax.experimental.pallas import tpu as pltpu
from jax.sharding import PartitionSpec as P

GAMMA_LESS = 0.4
UNIVERSAL_R = 0.25
TIME_STEP = 0.25
SECTION_DECAY = -0.4178904745
SECTION_WEIGHT = 0.3792103129
GRAD_FLOOR = 0.1
PROGRESS_SCALE = 4.0
CENTRAL_WEIGHTS = (0.8, -0.2, 4.0 / 105.0, -1.0 / 280.0)
WHOLE_WEIGHTS = (672.0, -168.0, 32.0, -3.0)
WHOLE_SCALE = 1.0 / 840.0
MOLAR_MASS = (2.0, 32.0, 16.0, 17.0, 18.0, 1.0, 33.0, 34.0, 28.0)
FORMATION_HEAT = (0.0, 0.0, 2.0, 0.3, -1.5, 3.0, 0.1, -0.4, 0.0)
ARRHENIUS_LIST = (
    (5, 1, (2, 3), 40.0, 2.0),
    (2, 0, (5, 3), 30.0, 1.2),
    (3, 0, (5, 4), 25.0, 0.8),
    (2, 4, (3, 3), 10.0, 1.6),
    (5, 1, (6,), 15.0, 0.2),
    (6, 5, (3, 3), 20.0, 0.3),
    (6, 6, (7, 1), 12.0, 0.4),
    (7, 8, (3, 3, 8), 8.0, 1.8),
)
FIELDS = 14
FLOWS = 5
LAYERS = 4 * FIELDS + FLOWS
FIRST = 5
MIB = 1 << 20
LONG = pl.CostEstimate(flops=10**10, bytes_accessed=10**6, transcendentals=0)
F32 = jnp.float32
BF16 = jnp.bfloat16


def make_table():
    table = np.zeros((14, 8))
    for column, step in enumerate(ARRHENIUS_LIST):
        change = np.zeros(9)
        change[step[0]] -= 1.0
        change[step[1]] -= 1.0
        for product in step[2]:
            change[product] += 1.0
        for species in range(9):
            mass_change = MOLAR_MASS[species] / 18.0 * change[species]
            table[5 + species, column] = mass_change
            table[4, column] -= FORMATION_HEAT[species] * mass_change
    return table


def ring(axis, distance):
    count = lax.axis_size(axis)
    return [(i, (i + distance) % count) for i in range(count)]


def lane_cell(lane):
    place = lane % 64
    return place % 4 if place < 4 * FIELDS else 0


def face_matrix():
    weights = np.zeros((128, 128), np.float32)
    for lane in range(64):
        cell = lane_cell(lane)
        for k in range(4 - cell):
            weights[k, lane] = WHOLE_WEIGHTS[k + cell]
            weights[127 - k, 64 + lane] = -WHOLE_WEIGHTS[k + cell]
    return np.concatenate([weights, weights], axis=0)


def place_matrix():
    weights = np.zeros((128, 128), np.float32)
    for lane in range(64):
        cell = lane_cell(lane)
        weights[lane, 127 - cell] = 1.0
        weights[64 + lane, cell] = 1.0
    return weights


def line_matrix():
    weights = np.zeros((128, 128), np.float32)
    for out in range(128):
        for m in range(1, 5):
            if out + m < 128:
                weights[out + m, out] = WHOLE_WEIGHTS[m - 1]
            if out - m >= 0:
                weights[out - m, out] = -WHOLE_WEIGHTS[m - 1]
    return np.concatenate([weights, weights], axis=0)


def planes_matrix():
    weights = np.zeros((128, 128), np.float32)
    for out in range(128):
        for m in range(1, 5):
            if out % 16 + m < 16:
                weights[out, out + m] = WHOLE_WEIGHTS[m - 1]
            if out % 16 - m >= 0:
                weights[out, out - m] = -WHOLE_WEIGHTS[m - 1]
    return np.concatenate([weights, weights], axis=1)


def lane_mask(field):
    lanes = lax.broadcasted_iota(jnp.int32, (1, 128), 1) % 64
    mask = (lanes >= 4 * field) & (lanes < 4 * field + 4)
    if field < FLOWS:
        mask = mask | (lanes == 4 * FIELDS + field)
    return mask


def two_terms(value):
    high = value.astype(BF16)
    low = (value - high.astype(F32)).astype(BF16)
    return high, low


def in_vmem(count):
    return [pl.BlockSpec(memory_space=pltpu.VMEM)] * count


def in_hbm(count):
    return [pl.BlockSpec(memory_space=pltpu.HBM)] * count


def far_kernel(count, fields_ref, *refs):
    far = count - 3
    blocks, (held, arrived) = refs[:far], refs[far:]
    depth = fields_ref.shape[1] // 16
    own = depth // count
    me = lax.axis_index("gy")
    copies = []
    for slot in range(far):
        first = own * lax.rem(me + slot + 2, count)
        for part, (begin, to, size) in enumerate(((first + depth - 2, 0, 2), (first, 2, own), (first + own, own + 2, 2))):
            source = pl.ds(pl.multiple_of(lax.rem(begin, depth) * 16, 16), size * 16)
            target = pl.ds(to * 16, size * 16)
            for index, (low, high, place) in enumerate(((0, 4, 0), (9, 10, 4))):
                copy = pltpu.make_async_copy(
                    fields_ref.at[low:high, source, :],
                    held.at[slot, place : place + high - low, target, :],
                    arrived.at[slot, part, index],
                )
                copy.start()
                copies.append(copy)
    for slot in range(far):
        for copy in copies[6 * slot : 6 * slot + 6]:
            copy.wait()
        planes = (own + 4) * 16
        for at in range(0, planes, 64):
            size = min(64, planes - at)
            rows = slice(at, at + size)
            density = held[slot, 0, rows, :]
            scalar = PROGRESS_SCALE * (held[slot, 4, rows, :] / density)
            blocks[slot][rows, :] = scalar.astype(BF16)
        for c in range(1, 4):
            base = planes + (c - 1) * (own + 2) * 16 - 16
            for at in range(16, planes - 16, 32):
                rows = slice(at, min(at + 32, planes - 16))
                speed = held[slot, c, rows, :] / held[slot, 0, rows, :]
                blocks[slot][base + rows.start : base + rows.stop, :] = speed.astype(BF16)


def far_part(fields, count):
    rows = fields.shape[1]
    own = rows // 16 // count
    far = count - 3
    return pl.pallas_call(
        functools.partial(far_kernel, count),
        in_specs=in_hbm(1),
        out_specs=in_vmem(far),
        out_shape=[jax.ShapeDtypeStruct(((4 * own + 10) * 16, 128), BF16)] * far,
        scratch_shapes=[
            pltpu.VMEM((far, 5, (own + 4) * 16, 128), F32),
            pltpu.SemaphoreType.DMA((far, 3, 2)),
        ],
        compiler_params=pltpu.CompilerParams(vmem_limit_bytes=52 * MIB),
        cost_estimate=LONG,
        name="far_part",
    )(fields)


def probe_kernel(count, fields_ref, prim, *refs):
    blocks, (held, progress, arrived) = refs[:3], refs[3:]
    rows = prim.shape[1]
    depth = rows // 16
    own = depth // count
    chunk = 256

    def arrival(step):
        there = pl.ds(pl.multiple_of(step * chunk, chunk), chunk)
        return [
            pltpu.make_async_copy(
                fields_ref.at[0:5, there, :], held.at[0:5, there, :], arrived.at[0, step]
            ),
            pltpu.make_async_copy(
                fields_ref.at[9, there, :], held.at[5, there, :], arrived.at[1, step]
            ),
        ]

    for step in range(rows // chunk):
        for copy in arrival(step):
            copy.start()

    def chunk_body(step, carry):
        for copy in arrival(step):
            copy.wait()

        def fill(part, inner_carry):
            at = pl.ds(pl.multiple_of(step * chunk + part * 64, 64), 64)
            density = held[0, at, :]
            mx, my, mz, energy = [held[c, at, :] for c in range(1, 5)]
            u, v, w = mx / density, my / density, mz / density
            stress = GAMMA_LESS * (energy - 0.5 * (mx * u + my * v + mz * w))
            progress[at, :] = PROGRESS_SCALE * (held[5, at, :] / density)
            prim[0, at, :] = u
            prim[1, at, :] = v
            prim[2, at, :] = w
            prim[3, at, :] = stress
            prim[4, at, :] = energy + stress
            return inner_carry

        lax.fori_loop(0, chunk // 64, fill, 0)
        return carry

    lax.fori_loop(0, rows // chunk, chunk_body, 0)

    me = lax.axis_index("gy")
    for block, distance in zip(blocks, (0, 1, count - 1)):
        first = own * lax.rem(me + distance, count) + depth
        offset = 0
        for c in range(4):
            margin = 2 if c == 0 else 1
            for z in range(-margin, own + margin):
                at = pl.ds(pl.multiple_of(lax.rem(first + z, depth) * 16, 16), 16)
                plane = progress[at, :] if c == 0 else prim[c - 1, at, :]
                block[offset : offset + 16, :] = plane.astype(BF16)
                offset += 16


def probe_part(fields, count):
    rows = fields.shape[1]
    own = rows // 16 // count
    main_rows = (4 * own + 10) * 16
    return pl.pallas_call(
        functools.partial(probe_kernel, count),
        in_specs=in_hbm(1),
        out_specs=in_vmem(4),
        out_shape=[jax.ShapeDtypeStruct((5, rows, 128), F32)]
        + [jax.ShapeDtypeStruct((main_rows, 128), BF16)] * 3,
        scratch_shapes=[
            pltpu.VMEM((6, rows, 128), F32),
            pltpu.VMEM((rows, 128), F32),
            pltpu.SemaphoreType.DMA((2, rows // 256)),
        ],
        compiler_params=pltpu.CompilerParams(vmem_limit_bytes=48 * MIB),
        cost_estimate=LONG,
        name="probe_part",
    )(fields)


def faces_kernel(flat, prim, low_ref, high_ref):
    rows = flat.shape[1]

    def chunk_body(step, carry):
        planes = pl.ds(pl.multiple_of(step * 16, 16), 16)

        def layer(ref, index, x):
            return ref[index, pl.ds(step * 256 + x, 16, stride=16), :]

        for ref, layers, sign in ((low_ref, (0, 1, 2, 3), 1.0), (high_ref, (15, 14, 13, 12), -1.0)):
            speeds = [layer(prim, 0, x) for x in layers]
            for field in range(FIELDS):
                source = (prim, 4) if field == 4 else (flat, field)
                flux = [layer(*source, x) * speeds[k] for k, x in enumerate(layers)]
                if field == 1:
                    flux = [flux[k] + layer(prim, 3, x) for k, x in enumerate(layers)]
                for cell in range(4):
                    part = (sign * CENTRAL_WEIGHTS[cell]) * flux[0]
                    for k in range(1, 4 - cell):
                        part = part + (sign * CENTRAL_WEIGHTS[k + cell]) * flux[k]
                    high, low = two_terms(part)
                    ref[4 * field + cell, planes, :] = high
                    if cell == 0 and field < FLOWS:
                        ref[4 * FIELDS + field, planes, :] = low
        return carry

    lax.fori_loop(0, rows // 256, chunk_body, 0)


def faces_part(fields, prim):
    rows = fields.shape[1]
    depth = rows // 16
    return pl.pallas_call(
        faces_kernel,
        in_specs=in_vmem(2),
        out_specs=in_vmem(2),
        out_shape=[jax.ShapeDtypeStruct((LAYERS, depth, 128), BF16)] * 2,
        compiler_params=pltpu.CompilerParams(vmem_limit_bytes=4 * MIB),
        cost_estimate=LONG,
        name="faces_part",
    )(fields, prim)


def lines_kernel(flat, prim, weights_ref, low_block, high_block, terms, low_ref, high_ref, total):
    start = low_block.shape[0]
    low_ref[0:start, :] = low_block[...]
    high_ref[0:start, :] = high_block[...]
    rows = flat.shape[1]
    half = rows // 2

    def fill(step, carry):
        at = pl.ds(pl.multiple_of(step * 32, 32), 32)
        v = prim[1, at, :]
        for field in range(FIELDS):
            flux = (prim[4, at, :] if field == 4 else flat[field, at, :]) * v
            if field == 2:
                flux = flux + prim[3, at, :]
            high, low = two_terms(flux)
            terms[field, at, 0:128] = high
            terms[field, at, 128:256] = low
        return carry

    lax.fori_loop(0, rows // 32, fill, 0)
    weights = weights_ref[...]
    for field in range(FIELDS):
        product = jnp.dot(terms[field], weights, preferred_element_type=F32)
        if field == 0:
            total[...] = product
        else:
            total[...] = jnp.where(lane_mask(field), product, total[...])
    value = total[...] * WHOLE_SCALE
    lanes = lax.broadcasted_iota(jnp.int32, (1, 128), 1)
    second = lanes % 64 >= 4 * FIELDS
    value = jnp.where(second, value - value.astype(BF16).astype(F32), value)
    turned = pltpu.roll(value, 64, 1)
    low_ref[start:, :] = jnp.where(lanes < 64, value[0:half, :], turned[half:rows, :]).astype(BF16)
    high_ref[start:, :] = jnp.where(lanes < 64, turned[0:half, :], value[half:rows, :]).astype(BF16)


def lines_part(flat, prim, low_block, high_block):
    rows = flat.shape[1]
    message = low_block.shape[0] + rows // 2
    return pl.pallas_call(
        lines_kernel,
        in_specs=in_vmem(5),
        out_specs=in_vmem(3),
        out_shape=[
            jax.ShapeDtypeStruct((FIELDS, rows, 256), BF16),
            jax.ShapeDtypeStruct((message, 128), BF16),
            jax.ShapeDtypeStruct((message, 128), BF16),
        ],
        scratch_shapes=[pltpu.VMEM((rows, 128), F32)],
        compiler_params=pltpu.CompilerParams(vmem_limit_bytes=12 * MIB),
        cost_estimate=LONG,
        name="lines_part",
    )(flat, prim, jnp.asarray(face_matrix(), BF16), low_block, high_block)


def sources(species, stress):
    moles = [species[k] * (18.0 / MOLAR_MASS[k]) for k in range(9)]
    summed = moles[0]
    for k in range(1, 9):
        summed = summed + moles[k]
    inverse_heat = UNIVERSAL_R * summed / stress
    e02 = jnp.exp(-0.2 * inverse_heat)
    e03 = jnp.exp(-0.3 * inverse_heat)
    e04 = e02 * e02
    e08 = e04 * e04
    e16 = e08 * e08
    powers = {0.2: e02, 0.3: e03, 0.4: e04, 0.8: e08, 1.6: e16}
    powers[1.2] = e08 * e04
    powers[1.8] = e16 * e02
    powers[2.0] = e16 * e04
    rates = [
        (step[3] * powers[step[4]]) * (moles[step[0]] * moles[step[1]]) for step in ARRHENIUS_LIST
    ]
    table = make_table()
    result = []
    for field in range(FIELDS):
        value = None
        for column in range(8):
            factor = float(table[field, column])
            if factor != 0.0:
                term = (TIME_STEP * factor) * rates[column]
                value = term if value is None else value + term
        result.append(value)
    return result


def windowed(flux, first, planes):
    window = {z: flux(z) for z in range(first - 4, first + 4)}
    for z in range(first, first + planes):
        window[z + 4] = flux(z + 4)
        change = None
        for m, weight in enumerate(CENTRAL_WEIGHTS, 1):
            term = (-TIME_STEP * weight) * (window[z + m] - window[z - m])
            change = term if change is None else change + term
        yield z, change


def inner_kernel(flat, prim, register, terms, line_ref, planes_ref, out, along_y):
    rows = flat.shape[1]
    depth = rows // 16

    def react(step, carry):
        at = pl.ds(pl.multiple_of(step * 32, 32), 32)
        made = sources([flat[5 + k, at, :] for k in range(9)], prim[3, at, :])
        for field in range(FIELDS):
            kept = SECTION_DECAY * register[field, at, :]
            out[field, at, :] = kept if made[field] is None else kept + made[field]
        return carry

    lax.fori_loop(0, rows // 32, react, 0)

    def along_x(flux):
        high, low = two_terms(flux)
        return jnp.dot(planes_ref[...], jnp.concatenate([high, low], axis=0), preferred_element_type=F32)

    def spread(field, carried):
        along_y[...] = jnp.dot(terms[field], line_ref[...], preferred_element_type=F32)
        for first in range(0, depth, 8):
            at = slice(first * 16, first * 16 + 128)
            both = along_y[at, :] + along_x(carried(at) * prim[0, at, :])
            out[field, at, :] += (-TIME_STEP * WHOLE_SCALE) * both
        for first in range(0, depth, 16):
            for row in (0, 8):

                def flux_z(z):
                    at = (z % depth) * 16 + row
                    return carried(slice(at, at + 8)) * prim[2, at : at + 8, :]

                for z, change in windowed(flux_z, first, 16):
                    at = slice(z * 16 + row, z * 16 + row + 8)
                    out[field, at, :] += change

    def across(index, carry):
        field = index + (index >= 4).astype(jnp.int32)
        spread(field, lambda at: flat[field, at, :])
        return carry

    lax.fori_loop(0, FIELDS - 1, across, 0)
    spread(4, lambda at: prim[4, at, :])

    for first in range(0, depth, 8):
        at = slice(first * 16, first * 16 + 128)
        out[1, at, :] += (-TIME_STEP * WHOLE_SCALE) * along_x(prim[3, at, :])
    for first in range(0, depth, 16):
        for row in (0, 8):

            def stress(z):
                at = (z % depth) * 16 + row
                return prim[3, at : at + 8, :]

            for z, change in windowed(stress, first, 16):
                at = slice(z * 16 + row, z * 16 + row + 8)
                out[3, at, :] += change


def inner_part(flat, prim, register, terms):
    rows = flat.shape[1]
    return pl.pallas_call(
        inner_kernel,
        in_specs=in_vmem(6),
        out_specs=pl.BlockSpec(memory_space=pltpu.VMEM),
        out_shape=jax.ShapeDtypeStruct((FIELDS, rows, 128), F32),
        scratch_shapes=[
            pltpu.VMEM((rows, 128), F32),
        ],
        compiler_params=pltpu.CompilerParams(vmem_limit_bytes=12 * MIB),
        cost_estimate=LONG,
        name="inner_part",
    )(flat, prim, register, terms, jnp.asarray(line_matrix(), BF16), jnp.asarray(planes_matrix(), BF16))


def add_faces(
    chosen, part, flat, prev, following, yprev, ynext, place_ref, fields_out, register_out,
    faces_x, along_y, message, fields_stage, register_stage, sent,
):
    rows = part.shape[1]
    depth = rows // 16
    half = rows // 2
    lanes = lax.broadcasted_iota(jnp.int32, (1, 128), 1)
    start = ynext.shape[0] - half
    low = ynext[start:, :].astype(F32)
    high = yprev[start:, :].astype(F32)
    message[0:half, :] = jnp.where(lanes < 64, low, pltpu.roll(high, 64, 1)).astype(BF16)
    message[half:rows, :] = jnp.where(lanes < 64, pltpu.roll(low, 64, 1), high).astype(BF16)
    faces_x[...] = jnp.zeros(faces_x.shape, F32)
    place = place_ref[...]
    copies = []
    for slot, field in enumerate(chosen):
        for ref, layers in ((prev, (0, 1, 2, 3)), (following, (15, 14, 13, 12))):
            for cell, x in enumerate(layers):
                value = ref[4 * field + cell, :, :].astype(F32)
                if cell == 0 and field < FLOWS:
                    value = value + ref[4 * FIELDS + field, :, :].astype(F32)
                faces_x[pl.ds(x, depth, stride=16), :] = value
        held = message[...]
        picked = jnp.where(lane_mask(field), held, jnp.zeros_like(held))
        along_y[...] = jnp.dot(picked, place, preferred_element_type=F32)
        stored = part[field] - TIME_STEP * (along_y[...] + faces_x[...])
        register_stage[slot] = stored
        fields_stage[slot] = flat[field] + SECTION_WEIGHT * stored
        for index, (stage, ref) in enumerate(((register_stage, register_out), (fields_stage, fields_out))):
            copy = pltpu.make_async_copy(stage.at[slot], ref.at[field], sent.at[index, slot])
            copy.start()
            copies.append(copy)
    return copies


def faces_scratch(number, rows):
    return [
        pltpu.VMEM((rows, 128), F32),
        pltpu.VMEM((rows, 128), F32),
        pltpu.VMEM((rows, 128), BF16),
        pltpu.VMEM((number, rows, 128), F32),
        pltpu.VMEM((number, rows, 128), F32),
        pltpu.SemaphoreType.DMA((2, number)),
    ]


def outer_kernel(chosen, *refs):
    for copy in add_faces(chosen, *refs):
        copy.wait()


def outer_part(chosen, operands):
    rows = operands[0].shape[1]
    return pl.pallas_call(
        functools.partial(outer_kernel, chosen),
        in_specs=in_vmem(7),
        out_specs=in_hbm(2),
        out_shape=[jax.ShapeDtypeStruct((FIELDS, rows, 128), F32)] * 2,
        scratch_shapes=faces_scratch(len(chosen), rows),
        compiler_params=pltpu.CompilerParams(vmem_limit_bytes=12 * MIB),
        cost_estimate=LONG,
        name="outer_part",
    )(*operands)


def lane_difference(values):
    lanes = lax.broadcasted_iota(jnp.int32, values[0].shape, 1)
    ahead = [pltpu.roll(value, 127, 1) for value in values]
    behind = [pltpu.roll(value, 1, 1) for value in values]
    count = len(values)
    return [
        jnp.where(lanes == 127, ahead[(j + 1) % count], ahead[j])
        - jnp.where(lanes == 0, behind[(j - 1) % count], behind[j])
        for j in range(count)
    ]


def in_pairs(total, work):
    together = 2 if total % 2 == 0 else 1

    def body(step, carry):
        for offset in range(together):
            work(step * together + offset)
        return carry

    lax.fori_loop(0, total // together, body, 0)


def inverse_length(a, b, c):
    return 1.0 * lax.rsqrt(jnp.maximum(a * a + b * b + c * c, GRAD_FLOOR * GRAD_FLOOR))


def unpack_kernel(count, own, *refs):
    blocks, (scalar, speed, low_ref, high_ref, edge) = refs[:count], refs[count:]
    edge[...] = jnp.zeros(edge.shape, F32)
    me = lax.axis_index("gy")
    for distance, block in enumerate(blocks):
        j = lax.rem(me - distance + count, count)
        for z in range(own + 4):
            scalar[j, z * 32 + 8 : z * 32 + 24, :] = block[z * 16 : z * 16 + 16, :].astype(F32)
        for c in range(3):
            base = (own + 4 + c * (own + 2)) * 16
            for z in range(own + 2):
                speed[c, j, z * 32 + 8 : z * 32 + 24, :] = block[
                    base + z * 16 : base + z * 16 + 16, :
                ].astype(F32)
        for ref, first, second in ((low_ref, 8, 9), (high_ref, 23, 22)):
            edge[0 : own + 2, :] = scalar[j, pl.ds(32 + first, own + 2, stride=32), :]
            edge[own + 2 : 2 * own + 2, :] = scalar[j, pl.ds(64 + second, own, stride=32), :]
            for c in range(3):
                start = (c + 2) * own + 2
                edge[start : start + own, :] = speed[c, j, pl.ds(32 + first, own, stride=32), :]
            ref[j, :, :] = edge[...].astype(BF16)


def unpack_part(blocks, own):
    count = len(blocks)
    edge_rows = -(-(5 * own + 2) // 16) * 16
    return pl.pallas_call(
        functools.partial(unpack_kernel, count, own),
        in_specs=in_vmem(count),
        out_specs=in_vmem(4),
        out_shape=[
            jax.ShapeDtypeStruct((count, (own + 4) * 32, 128), F32),
            jax.ShapeDtypeStruct((3, count, (own + 2) * 32, 128), F32),
            jax.ShapeDtypeStruct((count, edge_rows, 128), BF16),
            jax.ShapeDtypeStruct((count, edge_rows, 128), BF16),
        ],
        scratch_shapes=[pltpu.VMEM((edge_rows, 128), F32)],
        compiler_params=pltpu.CompilerParams(vmem_limit_bytes=4 * MIB),
        cost_estimate=LONG,
        name="unpack_part",
    )(*blocks)


def finish_kernel(count, own, chosen, *refs):
    operands, refs = refs[:7], refs[7:]
    scalar_in, speed_in, prev, following, _, _ = refs[:6]
    fields_out, register_out, scalar, speed, out_ref = refs[6:11]
    scratch, (normal, normal_z, edge, stage, sent) = refs[11:17], refs[17:]
    copies = add_faces(chosen, *operands, fields_out, register_out, *scratch)
    half = prev.shape[1]
    edge[:, 0:half, :] = prev[...].astype(F32)
    edge[:, half:, :] = following[...].astype(F32)
    for j in range(count):
        for side, row in ((0, 7), (half, 24)):
            scalar[j, pl.ds(32 + row, own + 2, stride=32), :] = edge[j, side : side + own + 2, :]
            for c in range(3):
                start = side + (c + 2) * own + 2
                speed[c, j, pl.ds(32 + row, own, stride=32), :] = edge[j, start : start + own, :]

    for side, inside, row in ((0, 8, 7), (half, 23, 24)):
        sign = 0.5 if row == 7 else -0.5
        lines = [edge[j, side + 1 : side + 1 + own, :] for j in range(count)]
        along_y = lane_difference(lines)
        for j in range(count):
            beyond = edge[j, side + own + 2 : side + 2 * own + 2, :]
            grad_x = sign * (scalar[j, pl.ds(64 + inside, own, stride=32), :] - beyond)
            grad_y = 0.5 * along_y[j]
            grad_z = 0.5 * (edge[j, side + 2 : side + 2 + own, :] - edge[j, side : side + own, :])
            normal[0, j, pl.ds(32 + row, own, stride=32), :] = -grad_x * inverse_length(
                grad_x, grad_y, grad_z
            )

    def window(z, row):
        return pl.ds(pl.multiple_of(z * 32, 32) + row, 16)

    def find_normals(z):
        along_y = lane_difference([scalar[j, window(z + 1, 8), :] for j in range(count)])
        for j in range(count):
            grad_x = 0.5 * (scalar[j, window(z + 1, 9), :] - scalar[j, window(z + 1, 7), :])
            grad_y = 0.5 * along_y[j]
            grad_z = 0.5 * (scalar[j, window(z + 2, 8), :] - scalar[j, window(z, 8), :])
            scale = -inverse_length(grad_x, grad_y, grad_z)
            normal[0, j, window(z, 8), :] = grad_x * scale
            normal[1, j, window(z, 8), :] = grad_y * scale
            normal_z[j, z, :, :] = grad_z * scale

    in_pairs(own + 2, find_normals)

    def find_metrics(z):
        curve_y = lane_difference([normal[1, j, window(z + 1, 8), :] for j in range(count)])
        speed_y = [
            lane_difference([speed[c, j, window(z + 1, 8), :] for j in range(count)])
            for c in range(3)
        ]
        for j in range(count):
            lanes = slice(j * 128, j * 128 + 128)
            normals = [
                normal[0, j, window(z + 1, 8), :],
                normal[1, j, window(z + 1, 8), :],
                normal_z[j, z + 1, :, :],
            ]
            curvature = 0.5 * (
                (normal[0, j, window(z + 1, 9), :] - normal[0, j, window(z + 1, 7), :])
                + curve_y[j]
                + (normal_z[j, z + 2, :, :] - normal_z[j, z, :, :])
            )
            strain = None
            for c in range(3):
                slopes = [
                    speed[c, j, window(z + 1, 9), :] - speed[c, j, window(z + 1, 7), :],
                    speed_y[c][j],
                    speed[c, j, window(z + 2, 8), :] - speed[c, j, window(z, 8), :],
                ]
                along = normals[0] * slopes[0] + normals[1] * slopes[1] + normals[2] * slopes[2]
                term = slopes[c] - normals[c] * along
                strain = term if strain is None else strain + term
            for index, value in enumerate(normals + [curvature, 0.5 * strain]):
                stage[index, z, :, lanes] = value.astype(BF16)
        pltpu.make_async_copy(stage.at[:, z], out_ref.at[:, z], sent.at[z]).start()

    in_pairs(own, find_metrics)
    for copy in copies:
        copy.wait()
    for z in range(own):
        pltpu.make_async_copy(stage.at[:, z], out_ref.at[:, z], sent.at[z]).wait()


def finish_part(chosen, operands, scalar, speed, prev, following, fields, register, own):
    count, half = prev.shape[:2]
    rows = fields.shape[1]
    shape = (5, own, 16, count * 128)
    fields, register, _, _, metrics = pl.pallas_call(
        functools.partial(finish_kernel, count, own, chosen),
        in_specs=in_vmem(11) + in_hbm(2),
        out_specs=in_hbm(2) + in_vmem(2) + in_hbm(1),
        out_shape=[
            jax.ShapeDtypeStruct(fields.shape, F32),
            jax.ShapeDtypeStruct(register.shape, F32),
            jax.ShapeDtypeStruct(scalar.shape, F32),
            jax.ShapeDtypeStruct(speed.shape, F32),
            jax.ShapeDtypeStruct(shape, BF16),
        ],
        input_output_aliases={7: 2, 8: 3, 11: 0, 12: 1},
        scratch_shapes=faces_scratch(len(chosen), rows)
        + [
            pltpu.VMEM((2, count, (own + 2) * 32, 128), F32),
            pltpu.VMEM((count, own + 2, 16, 128), F32),
            pltpu.VMEM((count, 2 * half, 128), F32),
            pltpu.VMEM(shape, BF16),
            pltpu.SemaphoreType.DMA((own,)),
        ],
        compiler_params=pltpu.CompilerParams(vmem_limit_bytes=20 * MIB),
        cost_estimate=LONG,
        name="finish_part",
    )(*operands, scalar, speed, prev, following, fields, register)
    return fields, register, metrics


def per_device(fields, register):
    depth, count_x, count_y = fields.shape[1:]
    flat = fields.reshape(FIELDS, depth * count_x, count_y)
    count = lax.axis_size("gy")
    own = depth // count
    x_forward, x_backward = ring("gx", 1), ring("gx", -1)

    blocks = [None] * count
    for slot, block in enumerate(far_part(flat, count)):
        blocks[slot + 2] = lax.ppermute(block, "gy", ring("gy", slot + 2))
    prim, blocks[0], blocks[1], blocks[count - 1] = probe_part(flat, count)
    low, high = faces_part(flat, prim)
    terms, to_prev, to_next = lines_part(flat, prim, blocks[count - 1], blocks[1])
    blocks[count - 1] = lax.ppermute(to_prev, "gy", ring("gy", -1))
    blocks[1] = lax.ppermute(to_next, "gy", ring("gy", 1))
    low, high, terms = lax.optimization_barrier((low, high, terms))
    following = lax.ppermute(low, "gx", x_backward)
    prev = lax.ppermute(high, "gx", x_forward)
    part = inner_part(flat, prim, register.reshape(flat.shape), terms)
    *blocks, part = lax.optimization_barrier((*blocks, part))
    scalar, speed, edge_low, edge_high = unpack_part(blocks, own)
    edge_prev = lax.ppermute(edge_high, "gx", x_forward)
    edge_next = lax.ppermute(edge_low, "gx", x_backward)
    part, scalar = lax.optimization_barrier((part, scalar))
    operands = (
        part, flat, prev, following, blocks[1], blocks[count - 1], jnp.asarray(place_matrix(), BF16)
    )
    first, last = tuple(range(FIRST)), tuple(range(FIRST, FIELDS))
    fields_next, register_next = outer_part(first, operands)
    edge_prev, edge_next, fields_next = lax.optimization_barrier((edge_prev, edge_next, fields_next))
    fields_next, register_next, metrics = finish_part(
        last, operands, scalar, speed, edge_prev, edge_next, fields_next, register_next, own
    )
    return (fields_next.reshape(fields.shape), register_next.reshape(fields.shape), metrics)


def solution(mesh):
    in_specs = (P(None, None, "gx", "gy"), P(None, None, "gx", "gy"))
    out_specs = (P(None, None, "gx", "gy"), P(None, None, "gx", "gy"), P(None, "gy", "gx", None))
    return jax.shard_map(
        per_device, mesh=mesh, in_specs=in_specs, out_specs=out_specs, check_vma=False
    )
```

```python
import functools

import jax
import jax.numpy as jnp
import numpy as np
from jax import lax
from jax.experimental import pallas as pl
from jax.experimental.pallas import tpu as pltpu
from jax.sharding import PartitionSpec as P

GAMMA_LESS = 0.4
UNIVERSAL_R = 0.25
TIME_STEP = 0.25
SECTION_DECAY = -0.4178904745
SECTION_WEIGHT = 0.3792103129
GRAD_FLOOR = 0.1
PROGRESS_SCALE = 4.0
CENTRAL_WEIGHTS = (0.8, -0.2, 4.0 / 105.0, -1.0 / 280.0)
WHOLE_WEIGHTS = (672.0, -168.0, 32.0, -3.0)
WHOLE_SCALE = 1.0 / 840.0
MOLAR_MASS = (2.0, 32.0, 16.0, 17.0, 18.0, 1.0, 33.0, 34.0, 28.0)
FORMATION_HEAT = (0.0, 0.0, 2.0, 0.3, -1.5, 3.0, 0.1, -0.4, 0.0)
ARRHENIUS_LIST = (
    (5, 1, (2, 3), 40.0, 2.0),
    (2, 0, (5, 3), 30.0, 1.2),
    (3, 0, (5, 4), 25.0, 0.8),
    (2, 4, (3, 3), 10.0, 1.6),
    (5, 1, (6,), 15.0, 0.2),
    (6, 5, (3, 3), 20.0, 0.3),
    (6, 6, (7, 1), 12.0, 0.4),
    (7, 8, (3, 3, 8), 8.0, 1.8),
)
FIELDS = 14
FLOWS = 5
LAYERS = 4 * FIELDS + FLOWS
FIRST = 4
MIB = 1 << 20
LONG = pl.CostEstimate(flops=10**10, bytes_accessed=10**6, transcendentals=0)
F32 = jnp.float32
BF16 = jnp.bfloat16


def make_table():
    table = np.zeros((14, 8))
    for column, step in enumerate(ARRHENIUS_LIST):
        change = np.zeros(9)
        change[step[0]] -= 1.0
        change[step[1]] -= 1.0
        for product in step[2]:
            change[product] += 1.0
        for species in range(9):
            mass_change = MOLAR_MASS[species] / 18.0 * change[species]
            table[5 + species, column] = mass_change
            table[4, column] -= FORMATION_HEAT[species] * mass_change
    return table


def ring(axis, distance):
    count = lax.axis_size(axis)
    return [(i, (i + distance) % count) for i in range(count)]


def lane_cell(lane):
    place = lane % 64
    return place % 4 if place < 4 * FIELDS else 0


def face_matrix():
    weights = np.zeros((128, 128), np.float32)
    for lane in range(64):
        cell = lane_cell(lane)
        for k in range(4 - cell):
            weights[k, lane] = WHOLE_WEIGHTS[k + cell]
            weights[127 - k, 64 + lane] = -WHOLE_WEIGHTS[k + cell]
    return np.concatenate([weights, weights], axis=0)


def place_matrix():
    weights = np.zeros((128, 128), np.float32)
    for lane in range(64):
        cell = lane_cell(lane)
        weights[lane, 127 - cell] = 1.0
        weights[64 + lane, cell] = 1.0
    return weights


def line_matrix():
    weights = np.zeros((128, 128), np.float32)
    for out in range(128):
        for m in range(1, 5):
            if out + m < 128:
                weights[out + m, out] = WHOLE_WEIGHTS[m - 1]
            if out - m >= 0:
                weights[out - m, out] = -WHOLE_WEIGHTS[m - 1]
    return np.concatenate([weights, weights], axis=0)


def planes_matrix():
    weights = np.zeros((128, 128), np.float32)
    for out in range(128):
        for m in range(1, 5):
            if out % 16 + m < 16:
                weights[out, out + m] = WHOLE_WEIGHTS[m - 1]
            if out % 16 - m >= 0:
                weights[out, out - m] = -WHOLE_WEIGHTS[m - 1]
    return np.concatenate([weights, weights], axis=1)


def lane_mask(field):
    lanes = lax.broadcasted_iota(jnp.int32, (1, 128), 1) % 64
    mask = (lanes >= 4 * field) & (lanes < 4 * field + 4)
    if field < FLOWS:
        mask = mask | (lanes == 4 * FIELDS + field)
    return mask


def two_terms(value):
    high = value.astype(BF16)
    low = (value - high.astype(F32)).astype(BF16)
    return high, low


def in_vmem(count):
    return [pl.BlockSpec(memory_space=pltpu.VMEM)] * count


def in_hbm(count):
    return [pl.BlockSpec(memory_space=pltpu.HBM)] * count


def far_kernel(count, fields_ref, *refs):
    far = count - 3
    blocks, (held, arrived) = refs[:far], refs[far:]
    depth = fields_ref.shape[1] // 16
    own = depth // count
    me = lax.axis_index("gy")
    copies = []
    for slot in range(far):
        first = own * lax.rem(me + slot + 2, count)
        for part, (begin, to, size) in enumerate(((first + depth - 2, 0, 2), (first, 2, own), (first + own, own + 2, 2))):
            source = pl.ds(pl.multiple_of(lax.rem(begin, depth) * 16, 16), size * 16)
            target = pl.ds(to * 16, size * 16)
            for index, (low, high, place) in enumerate(((0, 4, 0), (9, 10, 4))):
                copy = pltpu.make_async_copy(
                    fields_ref.at[low:high, source, :],
                    held.at[slot, place : place + high - low, target, :],
                    arrived.at[slot, part, index],
                )
                copy.start()
                copies.append(copy)
    for slot in range(far):
        for copy in copies[6 * slot : 6 * slot + 6]:
            copy.wait()
        planes = (own + 4) * 16
        for at in range(0, planes, 64):
            size = min(64, planes - at)
            rows = slice(at, at + size)
            density = held[slot, 0, rows, :]
            scalar = PROGRESS_SCALE * (held[slot, 4, rows, :] / density)
            blocks[slot][rows, :] = scalar.astype(BF16)
        for c in range(1, 4):
            base = planes + (c - 1) * (own + 2) * 16 - 16
            for at in range(16, planes - 16, 32):
                rows = slice(at, min(at + 32, planes - 16))
                speed = held[slot, c, rows, :] / held[slot, 0, rows, :]
                blocks[slot][base + rows.start : base + rows.stop, :] = speed.astype(BF16)


def far_part(fields, count):
    rows = fields.shape[1]
    own = rows // 16 // count
    far = count - 3
    return pl.pallas_call(
        functools.partial(far_kernel, count),
        in_specs=in_hbm(1),
        out_specs=in_vmem(far),
        out_shape=[jax.ShapeDtypeStruct(((4 * own + 10) * 16, 128), BF16)] * far,
        scratch_shapes=[
            pltpu.VMEM((far, 5, (own + 4) * 16, 128), F32),
            pltpu.SemaphoreType.DMA((far, 3, 2)),
        ],
        compiler_params=pltpu.CompilerParams(vmem_limit_bytes=52 * MIB),
        cost_estimate=LONG,
        name="far_part",
    )(fields)


def probe_kernel(count, fields_ref, prim, *refs):
    blocks, (held, progress, arrived) = refs[:3], refs[3:]
    rows = prim.shape[1]
    depth = rows // 16
    own = depth // count
    chunk = 256

    def arrival(step):
        there = pl.ds(pl.multiple_of(step * chunk, chunk), chunk)
        return [
            pltpu.make_async_copy(
                fields_ref.at[0:5, there, :], held.at[0:5, there, :], arrived.at[0, step]
            ),
            pltpu.make_async_copy(
                fields_ref.at[9, there, :], held.at[5, there, :], arrived.at[1, step]
            ),
        ]

    for step in range(rows // chunk):
        for copy in arrival(step):
            copy.start()

    def chunk_body(step, carry):
        for copy in arrival(step):
            copy.wait()

        def fill(part, inner_carry):
            at = pl.ds(pl.multiple_of(step * chunk + part * 64, 64), 64)
            density = held[0, at, :]
            mx, my, mz, energy = [held[c, at, :] for c in range(1, 5)]
            u, v, w = mx / density, my / density, mz / density
            stress = GAMMA_LESS * (energy - 0.5 * (mx * u + my * v + mz * w))
            progress[at, :] = PROGRESS_SCALE * (held[5, at, :] / density)
            prim[0, at, :] = u
            prim[1, at, :] = v
            prim[2, at, :] = w
            prim[3, at, :] = stress
            prim[4, at, :] = energy + stress
            return inner_carry

        lax.fori_loop(0, chunk // 64, fill, 0)
        return carry

    lax.fori_loop(0, rows // chunk, chunk_body, 0)

    me = lax.axis_index("gy")
    for block, distance in zip(blocks, (0, 1, count - 1)):
        first = own * lax.rem(me + distance, count) + depth
        offset = 0
        for c in range(4):
            margin = 2 if c == 0 else 1
            for z in range(-margin, own + margin):
                at = pl.ds(pl.multiple_of(lax.rem(first + z, depth) * 16, 16), 16)
                plane = progress[at, :] if c == 0 else prim[c - 1, at, :]
                block[offset : offset + 16, :] = plane.astype(BF16)
                offset += 16


def probe_part(fields, count):
    rows = fields.shape[1]
    own = rows // 16 // count
    main_rows = (4 * own + 10) * 16
    return pl.pallas_call(
        functools.partial(probe_kernel, count),
        in_specs=in_hbm(1),
        out_specs=in_vmem(4),
        out_shape=[jax.ShapeDtypeStruct((5, rows, 128), F32)]
        + [jax.ShapeDtypeStruct((main_rows, 128), BF16)] * 3,
        scratch_shapes=[
            pltpu.VMEM((6, rows, 128), F32),
            pltpu.VMEM((rows, 128), F32),
            pltpu.SemaphoreType.DMA((2, rows // 256)),
        ],
        compiler_params=pltpu.CompilerParams(vmem_limit_bytes=48 * MIB),
        cost_estimate=LONG,
        name="probe_part",
    )(fields)


def faces_kernel(flat, prim, low_ref, high_ref):
    rows = flat.shape[1]

    def chunk_body(step, carry):
        planes = pl.ds(pl.multiple_of(step * 16, 16), 16)

        def layer(ref, index, x):
            return ref[index, pl.ds(step * 256 + x, 16, stride=16), :]

        for ref, layers, sign in ((low_ref, (0, 1, 2, 3), 1.0), (high_ref, (15, 14, 13, 12), -1.0)):
            speeds = [layer(prim, 0, x) for x in layers]
            for field in range(FIELDS):
                source = (prim, 4) if field == 4 else (flat, field)
                flux = [layer(*source, x) * speeds[k] for k, x in enumerate(layers)]
                if field == 1:
                    flux = [flux[k] + layer(prim, 3, x) for k, x in enumerate(layers)]
                for cell in range(4):
                    part = (sign * CENTRAL_WEIGHTS[cell]) * flux[0]
                    for k in range(1, 4 - cell):
                        part = part + (sign * CENTRAL_WEIGHTS[k + cell]) * flux[k]
                    high, low = two_terms(part)
                    ref[4 * field + cell, planes, :] = high
                    if cell == 0 and field < FLOWS:
                        ref[4 * FIELDS + field, planes, :] = low
        return carry

    lax.fori_loop(0, rows // 256, chunk_body, 0)


def faces_part(fields, prim):
    rows = fields.shape[1]
    depth = rows // 16
    return pl.pallas_call(
        faces_kernel,
        in_specs=in_vmem(2),
        out_specs=in_vmem(2),
        out_shape=[jax.ShapeDtypeStruct((LAYERS, depth, 128), BF16)] * 2,
        compiler_params=pltpu.CompilerParams(vmem_limit_bytes=4 * MIB),
        cost_estimate=LONG,
        name="faces_part",
    )(fields, prim)


def lines_kernel(flat, prim, weights_ref, low_block, high_block, terms, low_ref, high_ref, total):
    start = low_block.shape[0]
    low_ref[0:start, :] = low_block[...]
    high_ref[0:start, :] = high_block[...]
    rows = flat.shape[1]
    half = rows // 2

    weights = weights_ref[...]

    def fill(step, carry):
        at = pl.ds(pl.multiple_of(step * 128, 128), 128)
        v = prim[1, at, :]
        chosen = None
        for field in range(FIELDS):
            flux = (prim[4, at, :] if field == 4 else flat[field, at, :]) * v
            if field == 2:
                flux = flux + prim[3, at, :]
            high, low = two_terms(flux)
            terms[field, at, 0:128] = high
            terms[field, at, 128:256] = low
            both = jnp.concatenate([high, low], axis=1)
            product = jnp.dot(both, weights, preferred_element_type=F32)
            chosen = product if chosen is None else jnp.where(lane_mask(field), product, chosen)
        total[at, :] = chosen
        return carry

    lax.fori_loop(0, rows // 128, fill, 0)
    value = total[...] * WHOLE_SCALE
    lanes = lax.broadcasted_iota(jnp.int32, (1, 128), 1)
    second = lanes % 64 >= 4 * FIELDS
    value = jnp.where(second, value - value.astype(BF16).astype(F32), value)
    turned = pltpu.roll(value, 64, 1)
    low_ref[start:, :] = jnp.where(lanes < 64, value[0:half, :], turned[half:rows, :]).astype(BF16)
    high_ref[start:, :] = jnp.where(lanes < 64, turned[0:half, :], value[half:rows, :]).astype(BF16)


def lines_part(flat, prim, low_block, high_block):
    rows = flat.shape[1]
    message = low_block.shape[0] + rows // 2
    return pl.pallas_call(
        lines_kernel,
        in_specs=in_vmem(5),
        out_specs=in_vmem(3),
        out_shape=[
            jax.ShapeDtypeStruct((FIELDS, rows, 256), BF16),
            jax.ShapeDtypeStruct((message, 128), BF16),
            jax.ShapeDtypeStruct((message, 128), BF16),
        ],
        scratch_shapes=[pltpu.VMEM((rows, 128), F32)],
        compiler_params=pltpu.CompilerParams(vmem_limit_bytes=12 * MIB),
        cost_estimate=LONG,
        name="lines_part",
    )(flat, prim, jnp.asarray(face_matrix(), BF16), low_block, high_block)


def sources(species, stress):
    moles = [species[k] * (18.0 / MOLAR_MASS[k]) for k in range(9)]
    summed = moles[0]
    for k in range(1, 9):
        summed = summed + moles[k]
    inverse_heat = UNIVERSAL_R * summed / stress
    e02 = jnp.exp(-0.2 * inverse_heat)
    e03 = jnp.exp(-0.3 * inverse_heat)
    e04 = e02 * e02
    e08 = e04 * e04
    e16 = e08 * e08
    powers = {0.2: e02, 0.3: e03, 0.4: e04, 0.8: e08, 1.6: e16}
    powers[1.2] = e08 * e04
    powers[1.8] = e16 * e02
    powers[2.0] = e16 * e04
    rates = [
        (step[3] * powers[step[4]]) * (moles[step[0]] * moles[step[1]]) for step in ARRHENIUS_LIST
    ]
    table = make_table()
    result = []
    for field in range(FIELDS):
        value = None
        for column in range(8):
            factor = float(table[field, column])
            if factor != 0.0:
                term = (TIME_STEP * factor) * rates[column]
                value = term if value is None else value + term
        result.append(value)
    return result


def windowed(flux, first, planes):
    window = {z: flux(z) for z in range(first - 4, first + 4)}
    for z in range(first, first + planes):
        window[z + 4] = flux(z + 4)
        change = None
        for m, weight in enumerate(CENTRAL_WEIGHTS, 1):
            term = (-TIME_STEP * weight) * (window[z + m] - window[z - m])
            change = term if change is None else change + term
        yield z, change


def inner_kernel(flat, prim, register, terms, line_ref, planes_ref, out, along_y):
    rows = flat.shape[1]
    depth = rows // 16

    def react(step, carry):
        at = pl.ds(pl.multiple_of(step * 32, 32), 32)
        made = sources([flat[5 + k, at, :] for k in range(9)], prim[3, at, :])
        for field in range(FIELDS):
            kept = SECTION_DECAY * register[field, at, :]
            out[field, at, :] = kept if made[field] is None else kept + made[field]
        return carry

    lax.fori_loop(0, rows // 32, react, 0)

    def along_x(flux):
        high, low = two_terms(flux)
        return jnp.dot(planes_ref[...], jnp.concatenate([high, low], axis=0), preferred_element_type=F32)

    def spread(field, carried):
        along_y[...] = jnp.dot(terms[field], line_ref[...], preferred_element_type=F32)
        for first in range(0, depth, 8):
            at = slice(first * 16, first * 16 + 128)
            both = along_y[at, :] + along_x(carried(at) * prim[0, at, :])
            out[field, at, :] += (-TIME_STEP * WHOLE_SCALE) * both
        for first in range(0, depth, 16):
            for row in (0, 8):

                def flux_z(z):
                    at = (z % depth) * 16 + row
                    return carried(slice(at, at + 8)) * prim[2, at : at + 8, :]

                for z, change in windowed(flux_z, first, 16):
                    at = slice(z * 16 + row, z * 16 + row + 8)
                    out[field, at, :] += change

    def across(index, carry):
        field = index + (index >= 4).astype(jnp.int32)
        spread(field, lambda at: flat[field, at, :])
        return carry

    lax.fori_loop(0, FIELDS - 1, across, 0)
    spread(4, lambda at: prim[4, at, :])

    for first in range(0, depth, 8):
        at = slice(first * 16, first * 16 + 128)
        out[1, at, :] += (-TIME_STEP * WHOLE_SCALE) * along_x(prim[3, at, :])
    for first in range(0, depth, 16):
        for row in (0, 8):

            def stress(z):
                at = (z % depth) * 16 + row
                return prim[3, at : at + 8, :]

            for z, change in windowed(stress, first, 16):
                at = slice(z * 16 + row, z * 16 + row + 8)
                out[3, at, :] += change


def inner_part(flat, prim, register, terms):
    rows = flat.shape[1]
    return pl.pallas_call(
        inner_kernel,
        in_specs=in_vmem(6),
        out_specs=pl.BlockSpec(memory_space=pltpu.VMEM),
        out_shape=jax.ShapeDtypeStruct((FIELDS, rows, 128), F32),
        scratch_shapes=[
            pltpu.VMEM((rows, 128), F32),
        ],
        compiler_params=pltpu.CompilerParams(vmem_limit_bytes=12 * MIB),
        cost_estimate=LONG,
        name="inner_part",
    )(flat, prim, register, terms, jnp.asarray(line_matrix(), BF16), jnp.asarray(planes_matrix(), BF16))


def add_faces(
    chosen, part, flat, prev, following, yprev, ynext, place_ref, fields_out, register_out,
    faces_x, along_y, message, fields_stage, register_stage, sent,
):
    rows = part.shape[1]
    depth = rows // 16
    half = rows // 2
    lanes = lax.broadcasted_iota(jnp.int32, (1, 128), 1)
    start = ynext.shape[0] - half
    low = ynext[start:, :].astype(F32)
    high = yprev[start:, :].astype(F32)
    message[0:half, :] = jnp.where(lanes < 64, low, pltpu.roll(high, 64, 1)).astype(BF16)
    message[half:rows, :] = jnp.where(lanes < 64, pltpu.roll(low, 64, 1), high).astype(BF16)
    faces_x[...] = jnp.zeros(faces_x.shape, F32)
    place = place_ref[...]
    copies = []
    for slot, field in enumerate(chosen):
        for ref, layers in ((prev, (0, 1, 2, 3)), (following, (15, 14, 13, 12))):
            for cell, x in enumerate(layers):
                value = ref[4 * field + cell, :, :].astype(F32)
                if cell == 0 and field < FLOWS:
                    value = value + ref[4 * FIELDS + field, :, :].astype(F32)
                faces_x[pl.ds(x, depth, stride=16), :] = value
        held = message[...]
        picked = jnp.where(lane_mask(field), held, jnp.zeros_like(held))
        along_y[...] = jnp.dot(picked, place, preferred_element_type=F32)
        stored = part[field] - TIME_STEP * (along_y[...] + faces_x[...])
        register_stage[slot] = stored
        fields_stage[slot] = flat[field] + SECTION_WEIGHT * stored
        for index, (stage, ref) in enumerate(((register_stage, register_out), (fields_stage, fields_out))):
            copy = pltpu.make_async_copy(stage.at[slot], ref.at[field], sent.at[index, slot])
            copy.start()
            copies.append(copy)
    return copies


def faces_scratch(number, rows):
    return [
        pltpu.VMEM((rows, 128), F32),
        pltpu.VMEM((rows, 128), F32),
        pltpu.VMEM((rows, 128), BF16),
        pltpu.VMEM((number, rows, 128), F32),
        pltpu.VMEM((number, rows, 128), F32),
        pltpu.SemaphoreType.DMA((2, number)),
    ]


def outer_kernel(chosen, *refs):
    for copy in add_faces(chosen, *refs):
        copy.wait()


def outer_part(chosen, operands):
    rows = operands[0].shape[1]
    return pl.pallas_call(
        functools.partial(outer_kernel, chosen),
        in_specs=in_vmem(7),
        out_specs=in_hbm(2),
        out_shape=[jax.ShapeDtypeStruct((FIELDS, rows, 128), F32)] * 2,
        scratch_shapes=faces_scratch(len(chosen), rows),
        compiler_params=pltpu.CompilerParams(vmem_limit_bytes=12 * MIB),
        cost_estimate=LONG,
        name="outer_part",
    )(*operands)


def lane_difference(values):
    lanes = lax.broadcasted_iota(jnp.int32, values[0].shape, 1)
    ahead = [pltpu.roll(value, 127, 1) for value in values]
    behind = [pltpu.roll(value, 1, 1) for value in values]
    count = len(values)
    return [
        jnp.where(lanes == 127, ahead[(j + 1) % count], ahead[j])
        - jnp.where(lanes == 0, behind[(j - 1) % count], behind[j])
        for j in range(count)
    ]


def in_pairs(total, work):
    together = 2 if total % 2 == 0 else 1

    def body(step, carry):
        for offset in range(together):
            work(step * together + offset)
        return carry

    lax.fori_loop(0, total // together, body, 0)


def inverse_length(a, b, c):
    return 1.0 * lax.rsqrt(jnp.maximum(a * a + b * b + c * c, GRAD_FLOOR * GRAD_FLOOR))


def unpack_kernel(count, own, *refs):
    blocks, (scalar, speed, low_ref, high_ref, edge) = refs[:count], refs[count:]
    edge[...] = jnp.zeros(edge.shape, F32)
    me = lax.axis_index("gy")
    for distance, block in enumerate(blocks):
        j = lax.rem(me - distance + count, count)
        for z in range(own + 4):
            scalar[j, z * 32 + 8 : z * 32 + 24, :] = block[z * 16 : z * 16 + 16, :].astype(F32)
        for c in range(3):
            base = (own + 4 + c * (own + 2)) * 16
            for z in range(own + 2):
                speed[c, j, z * 32 + 8 : z * 32 + 24, :] = block[
                    base + z * 16 : base + z * 16 + 16, :
                ].astype(F32)
        for ref, first, second in ((low_ref, 8, 9), (high_ref, 23, 22)):
            edge[0 : own + 2, :] = scalar[j, pl.ds(32 + first, own + 2, stride=32), :]
            edge[own + 2 : 2 * own + 2, :] = scalar[j, pl.ds(64 + second, own, stride=32), :]
            for c in range(3):
                start = (c + 2) * own + 2
                edge[start : start + own, :] = speed[c, j, pl.ds(32 + first, own, stride=32), :]
            ref[j, :, :] = edge[...].astype(BF16)


def unpack_part(blocks, own):
    count = len(blocks)
    edge_rows = -(-(5 * own + 2) // 16) * 16
    return pl.pallas_call(
        functools.partial(unpack_kernel, count, own),
        in_specs=in_vmem(count),
        out_specs=in_vmem(4),
        out_shape=[
            jax.ShapeDtypeStruct((count, (own + 4) * 32, 128), F32),
            jax.ShapeDtypeStruct((3, count, (own + 2) * 32, 128), F32),
            jax.ShapeDtypeStruct((count, edge_rows, 128), BF16),
            jax.ShapeDtypeStruct((count, edge_rows, 128), BF16),
        ],
        scratch_shapes=[pltpu.VMEM((edge_rows, 128), F32)],
        compiler_params=pltpu.CompilerParams(vmem_limit_bytes=4 * MIB),
        cost_estimate=LONG,
        name="unpack_part",
    )(*blocks)


def finish_kernel(count, own, chosen, *refs):
    operands, refs = refs[:7], refs[7:]
    scalar_in, speed_in, prev, following, _, _ = refs[:6]
    fields_out, register_out, scalar, speed, out_ref = refs[6:11]
    scratch, (normal, normal_z, edge, stage, sent) = refs[11:17], refs[17:]
    copies = add_faces(chosen, *operands, fields_out, register_out, *scratch)
    half = prev.shape[1]
    edge[:, 0:half, :] = prev[...].astype(F32)
    edge[:, half:, :] = following[...].astype(F32)
    for j in range(count):
        for side, row in ((0, 7), (half, 24)):
            scalar[j, pl.ds(32 + row, own + 2, stride=32), :] = edge[j, side : side + own + 2, :]
            for c in range(3):
                start = side + (c + 2) * own + 2
                speed[c, j, pl.ds(32 + row, own, stride=32), :] = edge[j, start : start + own, :]

    for side, inside, row in ((0, 8, 7), (half, 23, 24)):
        sign = 0.5 if row == 7 else -0.5
        lines = [edge[j, side + 1 : side + 1 + own, :] for j in range(count)]
        along_y = lane_difference(lines)
        for j in range(count):
            beyond = edge[j, side + own + 2 : side + 2 * own + 2, :]
            grad_x = sign * (scalar[j, pl.ds(64 + inside, own, stride=32), :] - beyond)
            grad_y = 0.5 * along_y[j]
            grad_z = 0.5 * (edge[j, side + 2 : side + 2 + own, :] - edge[j, side : side + own, :])
            normal[0, j, pl.ds(32 + row, own, stride=32), :] = -grad_x * inverse_length(
                grad_x, grad_y, grad_z
            )

    def window(z, row):
        return pl.ds(pl.multiple_of(z * 32, 32) + row, 16)

    def find_normals(z):
        along_y = lane_difference([scalar[j, window(z + 1, 8), :] for j in range(count)])
        for j in range(count):
            grad_x = 0.5 * (scalar[j, window(z + 1, 9), :] - scalar[j, window(z + 1, 7), :])
            grad_y = 0.5 * along_y[j]
            grad_z = 0.5 * (scalar[j, window(z + 2, 8), :] - scalar[j, window(z, 8), :])
            scale = -inverse_length(grad_x, grad_y, grad_z)
            normal[0, j, window(z, 8), :] = grad_x * scale
            normal[1, j, window(z, 8), :] = grad_y * scale
            normal_z[j, z, :, :] = grad_z * scale

    in_pairs(own + 2, find_normals)

    def find_metrics(z):
        curve_y = lane_difference([normal[1, j, window(z + 1, 8), :] for j in range(count)])
        speed_y = [
            lane_difference([speed[c, j, window(z + 1, 8), :] for j in range(count)])
            for c in range(3)
        ]
        for j in range(count):
            lanes = slice(j * 128, j * 128 + 128)
            normals = [
                normal[0, j, window(z + 1, 8), :],
                normal[1, j, window(z + 1, 8), :],
                normal_z[j, z + 1, :, :],
            ]
            curvature = 0.5 * (
                (normal[0, j, window(z + 1, 9), :] - normal[0, j, window(z + 1, 7), :])
                + curve_y[j]
                + (normal_z[j, z + 2, :, :] - normal_z[j, z, :, :])
            )
            strain = None
            for c in range(3):
                slopes = [
                    speed[c, j, window(z + 1, 9), :] - speed[c, j, window(z + 1, 7), :],
                    speed_y[c][j],
                    speed[c, j, window(z + 2, 8), :] - speed[c, j, window(z, 8), :],
                ]
                along = normals[0] * slopes[0] + normals[1] * slopes[1] + normals[2] * slopes[2]
                term = slopes[c] - normals[c] * along
                strain = term if strain is None else strain + term
            for index, value in enumerate(normals + [curvature, 0.5 * strain]):
                stage[index, z, :, lanes] = value.astype(BF16)
        pltpu.make_async_copy(stage.at[:, z], out_ref.at[:, z], sent.at[z]).start()

    in_pairs(own, find_metrics)
    for copy in copies:
        copy.wait()
    for z in range(own):
        pltpu.make_async_copy(stage.at[:, z], out_ref.at[:, z], sent.at[z]).wait()


def finish_part(chosen, operands, scalar, speed, prev, following, fields, register, own):
    count, half = prev.shape[:2]
    rows = fields.shape[1]
    shape = (5, own, 16, count * 128)
    fields, register, _, _, metrics = pl.pallas_call(
        functools.partial(finish_kernel, count, own, chosen),
        in_specs=in_vmem(11) + in_hbm(2),
        out_specs=in_hbm(2) + in_vmem(2) + in_hbm(1),
        out_shape=[
            jax.ShapeDtypeStruct(fields.shape, F32),
            jax.ShapeDtypeStruct(register.shape, F32),
            jax.ShapeDtypeStruct(scalar.shape, F32),
            jax.ShapeDtypeStruct(speed.shape, F32),
            jax.ShapeDtypeStruct(shape, BF16),
        ],
        input_output_aliases={7: 2, 8: 3, 11: 0, 12: 1},
        scratch_shapes=faces_scratch(len(chosen), rows)
        + [
            pltpu.VMEM((2, count, (own + 2) * 32, 128), F32),
            pltpu.VMEM((count, own + 2, 16, 128), F32),
            pltpu.VMEM((count, 2 * half, 128), F32),
            pltpu.VMEM(shape, BF16),
            pltpu.SemaphoreType.DMA((own,)),
        ],
        compiler_params=pltpu.CompilerParams(vmem_limit_bytes=20 * MIB),
        cost_estimate=LONG,
        name="finish_part",
    )(*operands, scalar, speed, prev, following, fields, register)
    return fields, register, metrics


def per_device(fields, register):
    depth, count_x, count_y = fields.shape[1:]
    flat = fields.reshape(FIELDS, depth * count_x, count_y)
    count = lax.axis_size("gy")
    own = depth // count
    x_forward, x_backward = ring("gx", 1), ring("gx", -1)

    blocks = [None] * count
    for slot, block in enumerate(far_part(flat, count)):
        blocks[slot + 2] = lax.ppermute(block, "gy", ring("gy", slot + 2))
    prim, blocks[0], blocks[1], blocks[count - 1] = probe_part(flat, count)
    low, high = faces_part(flat, prim)
    following = lax.ppermute(low, "gx", x_backward)
    prev = lax.ppermute(high, "gx", x_forward)
    terms, to_prev, to_next = lines_part(flat, prim, blocks[count - 1], blocks[1])
    blocks[count - 1] = lax.ppermute(to_prev, "gy", ring("gy", -1))
    blocks[1] = lax.ppermute(to_next, "gy", ring("gy", 1))
    part = inner_part(flat, prim, register.reshape(flat.shape), terms)
    *blocks, part = lax.optimization_barrier((*blocks, part))
    scalar, speed, edge_low, edge_high = unpack_part(blocks, own)
    edge_prev = lax.ppermute(edge_high, "gx", x_forward)
    edge_next = lax.ppermute(edge_low, "gx", x_backward)
    part, scalar = lax.optimization_barrier((part, scalar))
    operands = (
        part, flat, prev, following, blocks[1], blocks[count - 1], jnp.asarray(place_matrix(), BF16)
    )
    first, last = tuple(range(FIRST)), tuple(range(FIRST, FIELDS))
    fields_next, register_next = outer_part(first, operands)
    edge_prev, edge_next, fields_next = lax.optimization_barrier((edge_prev, edge_next, fields_next))
    fields_next, register_next, metrics = finish_part(
        last, operands, scalar, speed, edge_prev, edge_next, fields_next, register_next, own
    )
    return (fields_next.reshape(fields.shape), register_next.reshape(fields.shape), metrics)


def solution(mesh):
    in_specs = (P(None, None, "gx", "gy"), P(None, None, "gx", "gy"))
    out_specs = (P(None, None, "gx", "gy"), P(None, None, "gx", "gy"), P(None, "gy", "gx", None))
    return jax.shard_map(
        per_device, mesh=mesh, in_specs=in_specs, out_specs=out_specs, check_vma=False
    )
```
